256 devices in a mesh: seq: 64 (over x, z, y_lo), dp: 4 (over y_hi, core).
Axes of the slice: x: 4, y: 4 (y_hi: 2, y_lo: 2; y = y_hi * 2 + y_lo), z: 8, core: 2. Of those that a mesh axis runs over, the one named last changes fastest.
Arguments:
- tokens: bfloat16 [4, 8192, 1536], P('dp', 'seq'), may hold values from -16 to 16
- upstream: bfloat16 [4, 8192, 1536], P('dp', 'seq'), may hold values from -6 to 6
- w_query: bfloat16 [1536, 512], replicated, may hold values from -10 to 10, as said below
- w_keyval: bfloat16 [1536, 256], replicated, may hold values from -1 to 1, as said below
- w_out: bfloat16 [512, 1536], replicated, may hold values from -0.25 to 0.25
Outputs:
- attended: bfloat16 [4, 8192, 1536], P('dp', 'seq')
- grad_tokens: bfloat16 [4, 8192, 1536], P('dp', 'seq')
- grad_query: float32 [1536, 512], P('seq')
- grad_keyval: float32 [1536, 256], P('seq')
- grad_out: float32 [512, 1536], P('seq')
The draws below stay inside these ranges and needn't reach their ends.
Inputs may be any that keep to these rules, and one draw needn't show every extreme that they name: `w_query`: entries of order 1536 ** -0.5 times a modest factor. `w_keyval`: entries of order 1536 ** -0.5.
All inputs are finite; a program needn't handle non-finite values.
Results may differ from the reference program's by a relative error of at most 0.035.
The reference program's roundings to bfloat16 on the way (of `query`, `keyval`, `prob`, `mixed`, `dmixed`, `dscore`, `dquery` and `dkeyval`) count: a program that leaves them out, or rounds other values in their place, can miss the bound.
Values may be sent and summed in bfloat16 or wider, within the bound.
No kernel may reach another device: no remote copies, remote signals or barrier semaphores. Data moves between devices by JAX's collectives and lax.ppermute only.
A program may use at most 128 MiB of HBM per device.

```python
import jax
import jax.numpy as jnp
from jax import lax

D = 1536
HEADS = 4
HEAD_DIM = 128
SEQ_LEN = 8192
EXAMPLES = 4


def shared_keys(key):
    base = jnp.clip(jax.random.normal(key, (D, HEAD_DIM), jnp.float32), -6.0, 6.0)
    return base * D ** (-0.5)


def draw_w_query(key, part):
    key = jax.random.fold_in(key, 3)
    noise = jnp.clip(jax.random.normal(key, (D, HEADS, HEAD_DIM), jnp.float32), -6.0, 6.0) * D ** (-0.5)
    return noise.reshape(D, HEADS * HEAD_DIM).astype(jnp.bfloat16)


def draw_w_keyval(key, part):
    base = shared_keys(key)
    key = jax.random.fold_in(key, 5)
    values = jnp.clip(jax.random.normal(key, (D, HEAD_DIM), jnp.float32), -6.0, 6.0) * D ** (-0.5)
    return jnp.concatenate([base, values], axis=1).astype(jnp.bfloat16)


def spiked(entries, key, source, target, shards_of, factor):
    owner, partner = [(jnp.arange(entries.shape[position]) // (entries.shape[position] // shards_of)).reshape([-1 if axis == position else 1 for axis in range(entries.ndim)]) for position in (source, target)]
    chosen = jax.random.permutation(key, shards_of)[partner]
    strong = (owner == chosen) | (owner == (partner + shards_of // 2) % shards_of)
    return jnp.where(strong, factor * entries, entries)


def level_of(key, shape, pieces, least, top_value):
    def one(position, blocks):
        draws = jax.random.uniform(jax.random.fold_in(jax.random.fold_in(key, 6), position), (blocks,), jnp.float32, least / len(pieces), top_value / len(pieces))
        return jnp.repeat(jnp.exp(draws), shape[position] // blocks).reshape((-1,) + (1,) * (len(shape) - position - 1))

    loudness = one(*pieces[0])
    for cut in pieces[1:]:
        loudness = loudness * one(*cut)
    return loudness


def normal_values(key, extent, width, limit, split=(), held_as=jnp.bfloat16):
    values = jax.random.normal(key, extent, jnp.float32) * width
    if len(split) > 0:
        values = level_of(key, extent, split, -0.22, 0.18) * values
    return jnp.clip(values, min=-limit, max=limit).astype(held_as)


def gaussian_with(own_key, extent, deviation, limit, cuts, heavy, held_as=jnp.bfloat16):
    drawn = deviation * jax.random.normal(own_key, extent, jnp.float32)
    if cuts:
        drawn = drawn * level_of(own_key, extent, cuts, -0.22, 0.18)
    return jnp.clip(spiked(drawn, jax.random.fold_in(own_key, 3), *heavy), -limit, limit).astype(held_as)


def setup_inputs(seed: int = 0) -> dict:
    seeds = jax.random.split(jax.random.key(seed), 6)
    return {
        "tokens": gaussian_with(seeds[0], (EXAMPLES, SEQ_LEN, D), 1.0, 16.0, ((0, 4), (1, 64)), (1, 2, 64, 4.0)),
        "upstream": normal_values(seeds[1], (EXAMPLES, SEQ_LEN, D), 1.0, 6.0, ((0, 4), (1, 64))),
        "w_query": draw_w_query(jax.random.fold_in(seeds[5], 71), 0),
        "w_keyval": draw_w_keyval(jax.random.fold_in(seeds[5], 71), 0),
        "w_out": normal_values(seeds[4], (HEADS * HEAD_DIM, D), (HEADS * HEAD_DIM) ** -0.5, 0.25),
    }


def one_example(tokens_ex, upstream_ex, w_query, w_keyval, w_out):
    scale = 1.0 / (HEAD_DIM ** 0.5)
    query = jnp.dot(tokens_ex, w_query, preferred_element_type=jnp.float32).astype(jnp.bfloat16)
    keyval = jnp.dot(tokens_ex, w_keyval, preferred_element_type=jnp.float32).astype(jnp.bfloat16)
    keys = keyval[:, :HEAD_DIM].astype(jnp.float32)
    values = keyval[:, HEAD_DIM:].astype(jnp.float32)
    rows = min(512, SEQ_LEN)
    blocks = SEQ_LEN // rows
    query_blocks = query.reshape(blocks, rows, HEADS, HEAD_DIM)

    def forward_block(qblock):
        qf = qblock.astype(jnp.float32)
        score = jnp.einsum('rhd,kd->hrk', qf, keys) * scale
        top = jnp.max(score, axis=-1)
        weight = jnp.exp(score - top[..., None])
        total = jnp.sum(weight, axis=-1)
        prob = (weight / total[..., None]).astype(jnp.bfloat16)
        mixed = jnp.einsum('hrk,kd->rhd', prob.astype(jnp.float32), values)
        return mixed.reshape(rows, HEADS * HEAD_DIM).astype(jnp.bfloat16), top + jnp.log(total)

    mixed, logsum = lax.map(forward_block, query_blocks)
    mixed = mixed.reshape(SEQ_LEN, HEADS * HEAD_DIM)
    attended = (tokens_ex.astype(jnp.float32) + jnp.dot(mixed, w_out, preferred_element_type=jnp.float32)).astype(jnp.bfloat16)
    dmixed = jnp.dot(upstream_ex, w_out.T, preferred_element_type=jnp.float32).astype(jnp.bfloat16)
    delta = jnp.sum((dmixed.astype(jnp.float32) * mixed.astype(jnp.float32)).reshape(blocks, rows, HEADS, HEAD_DIM), axis=-1)
    delta = jnp.transpose(delta, (0, 2, 1))
    dmixed_blocks = dmixed.reshape(blocks, rows, HEADS, HEAD_DIM)

    def backward_block(carry, inputs):
        qblock, dblock, lblock, eblock = inputs
        qf = qblock.astype(jnp.float32)
        df = dblock.astype(jnp.float32)
        score = jnp.einsum('rhd,kd->hrk', qf, keys) * scale
        prob = jnp.exp(score - lblock[..., None])
        dprob = jnp.einsum('rhd,kd->hrk', df, values)
        dscore = (prob * (dprob - eblock[..., None]) * scale).astype(jnp.bfloat16).astype(jnp.float32)
        dquery = jnp.einsum('hrk,kd->rhd', dscore, keys).reshape(rows, HEADS * HEAD_DIM).astype(jnp.bfloat16)
        dkey = jnp.einsum('hrk,rhd->kd', dscore, qf)
        dvalue = jnp.einsum('hrk,rhd->kd', prob.astype(jnp.bfloat16).astype(jnp.float32), df)
        return carry + jnp.concatenate([dkey, dvalue], axis=1), dquery

    dkv_sum, dquery = lax.scan(backward_block, jnp.zeros((SEQ_LEN, 2 * HEAD_DIM), jnp.float32),
                               (query_blocks, dmixed_blocks, logsum, delta))
    dkeyval = dkv_sum.astype(jnp.bfloat16)
    dquery = dquery.reshape(SEQ_LEN, HEADS * HEAD_DIM)
    grad_tokens = (jnp.dot(dquery, w_query.T, preferred_element_type=jnp.float32)
                   + jnp.dot(dkeyval, w_keyval.T, preferred_element_type=jnp.float32)).astype(jnp.bfloat16)
    grad_q = jnp.dot(tokens_ex.T, dquery, preferred_element_type=jnp.float32)
    grad_kv = jnp.dot(tokens_ex.T, dkeyval, preferred_element_type=jnp.float32)
    grad_o = jnp.dot(mixed.T, upstream_ex, preferred_element_type=jnp.float32)
    return attended, grad_tokens, grad_q, grad_kv, grad_o


def reference(tokens, upstream, w_query, w_keyval, w_out):
    outputs = []
    gradients = []
    grad_q = jnp.zeros((D, HEADS * HEAD_DIM), jnp.float32)
    grad_kv = jnp.zeros((D, 2 * HEAD_DIM), jnp.float32)
    grad_o = jnp.zeros((HEADS * HEAD_DIM, D), jnp.float32)
    for example in range(EXAMPLES):
        attended, grad_tokens, part_q, part_kv, part_o = one_example(tokens[example], upstream[example], w_query, w_keyval, w_out)
        outputs.append(attended)
        gradients.append(grad_tokens)
        grad_q = grad_q + part_q
        grad_kv = grad_kv + part_kv
        grad_o = grad_o + part_o
    return jnp.stack(outputs), jnp.stack(gradients), grad_q, grad_kv, grad_o
```

```python
import math

import jax
import jax.numpy as jnp
from jax import lax
from jax.experimental import pallas as pl
from jax.experimental.pallas import tpu as pltpu
from jax.sharding import Mesh, PartitionSpec as P

HEADS = 4
HEAD_DIM = 128
POS = 128
ROWS = HEADS * POS
GROUP = 8
KEYS = 8 * POS
FORWARD_CHUNK = 512
BACKWARD_CHUNK = 128
SCALE = 1.0 / HEAD_DIM**0.5
LOG2E = math.log2(math.e)
AXES = ("x", "z", "yl", "yh", "core")
SEQ = ("x", "z", "yl")
DP = ("yh", "core")
NT = (((1,), (1,)), ((), ()))
TN = (((0,), (0,)), ((), ()))
F32 = jnp.float32
BF16 = jnp.bfloat16
VMEM_LIMIT = 56 * 1024 * 1024


def dot(a, b, dims=(((1,), (0,)), ((), ()))):
    return lax.dot_general(a, b, dims, preferred_element_type=F32)


def send(array, axis, size, step):
    return lax.ppermute(array, axis, [(i, (i + step) % size) for i in range(size)])


def rows_of(block):
    return jnp.concatenate(
        [block[:, h * HEAD_DIM : (h + 1) * HEAD_DIM] for h in range(HEADS)], axis=0
    )


def forward_kernel(qd, *refs):
    mixed, stats_ref, kv, vt, score = refs[8:]
    for i in range(8):
        kv[i * POS : (i + 1) * POS, :] = refs[i][...]
    vt[...] = kv[:, HEAD_DIM:].T

    def block(p, carry):
        both = qd[p]
        q4 = rows_of(both[:, :ROWS])
        d4 = rows_of(both[:, ROWS:])
        top = jnp.full((1, ROWS), -jnp.inf, F32)
        for c in range(KEYS // FORWARD_CHUNK):
            part = slice(c * FORWARD_CHUNK, (c + 1) * FORWARD_CHUNK)
            s = dot(kv[part, :HEAD_DIM], q4, NT)
            score[part, :] = s
            top = jnp.maximum(top, jnp.max(s, axis=0, keepdims=True))
        base = top * (SCALE * LOG2E)
        total = jnp.zeros((1, ROWS), F32)
        weighted = jnp.zeros((1, ROWS), F32)
        acc = jnp.zeros((HEAD_DIM, ROWS), F32)
        for c in range(KEYS // FORWARD_CHUNK):
            part = slice(c * FORWARD_CHUNK, (c + 1) * FORWARD_CHUNK)
            e = jnp.exp2(score[part, :] * (SCALE * LOG2E) - base)
            dp = dot(kv[part, HEAD_DIM:], d4, NT)
            total = total + jnp.sum(e, axis=0, keepdims=True)
            weighted = weighted + jnp.sum(e * dp, axis=0, keepdims=True)
            acc = acc + dot(vt[:, part], e.astype(BF16))
        inverse = 1.0 / total
        mixed[p] = (acc * inverse).astype(BF16)
        stats_ref[pl.ds(p, 1), :] = top * SCALE + jnp.log(total)
        stats_ref[pl.ds(8 + p, 1), :] = weighted * inverse
        return carry

    lax.fori_loop(0, GROUP, block, 0)


def combine(logs, bars):
    top = jnp.max(logs, axis=0)
    weights = jnp.exp(logs - top)
    total = jnp.sum(weights, axis=0)
    weights = weights / total
    return top + jnp.log(total), jnp.sum(weights * bars, axis=0), weights


def backward_kernel(qd, stats_ref, *refs):
    dq, dkv_out = refs[8], refs[9:17]
    kv, kt, stat, dkv = refs[17:]
    for i in range(8):
        kv[i * POS : (i + 1) * POS, :] = refs[i][...]
    kt[...] = kv[:, :HEAD_DIM].T
    logsum, delta, unused = combine(stats_ref[:, :8, :], stats_ref[:, 8:, :])
    stat[:8, :] = logsum * LOG2E
    stat[8:, :] = delta
    dkv[...] = jnp.zeros_like(dkv)

    def block(p, carry):
        both = qd[p]
        q4 = rows_of(both[:, :ROWS])
        d4 = rows_of(both[:, ROWS:])
        base = stat[pl.ds(p, 1), :]
        delta = stat[pl.ds(8 + p, 1), :]
        acc = jnp.zeros((HEAD_DIM, ROWS), F32)
        for c in range(KEYS // BACKWARD_CHUNK):
            part = slice(c * BACKWARD_CHUNK, (c + 1) * BACKWARD_CHUNK)
            s = dot(kv[part, :HEAD_DIM], q4, NT)
            prob = jnp.exp2(s * (SCALE * LOG2E) - base)
            dp = dot(kv[part, HEAD_DIM:], d4, NT)
            ds = (prob * (dp - delta)).astype(BF16)
            dkv[part, HEAD_DIM:] += dot(prob.astype(BF16), d4)
            dkv[part, :HEAD_DIM] += dot(ds, q4)
            acc = acc + dot(kt[:, part], ds)
        dq[p] = (acc * SCALE).astype(BF16)
        return carry

    lax.fori_loop(0, GROUP, block, 0)
    for i in range(8):
        part = slice(i * POS, (i + 1) * POS)
        dkv_out[i][:, :HEAD_DIM] = (dkv[part, :HEAD_DIM] * SCALE).astype(BF16)
        dkv_out[i][:, HEAD_DIM:] = dkv[part, HEAD_DIM:].astype(BF16)


def output_kernel(place, parts, stats_ref, tokens_ref, upstream_ref, w_out_ref, *outs):
    attended_ref, keep_ref, give_ref = outs
    mine = place[1]
    unused, unused, weights = combine(
        stats_ref[:, pl.ds(mine, 1), :], stats_ref[:, pl.ds(8 + mine, 1), :]
    )
    mixed_t = jnp.sum(weights * parts[...].astype(F32), axis=0)
    heads_t = [mixed_t[:, h * POS : (h + 1) * POS] for h in range(HEADS)]
    mixed = jnp.concatenate([m.T for m in heads_t], axis=1).astype(BF16)
    mixed_rows = jnp.concatenate(heads_t, axis=0).astype(BF16)
    attended_ref[...] = (
        tokens_ref[...].astype(F32) + dot(mixed, w_out_ref[...])
    ).astype(BF16)
    half = upstream_ref.shape[1] // 2
    first = place[0] == 0
    low, high = upstream_ref[:, :half], upstream_ref[:, half:]
    keep_ref[...] = dot(mixed_rows, jnp.where(first, low, high)).astype(BF16)
    give_ref[...] = dot(mixed_rows, jnp.where(first, high, low)).astype(BF16)


def input_kernel(place, dq_ref, *refs):
    dkv_refs = refs[:8]
    tokens_ref, w_query_ref, w_keyval_ref, grad_ref, keep_ref, give_ref = refs[8:]
    dq_t = jnp.sum(dq_ref[...].astype(F32), axis=0)
    dquery = jnp.concatenate(
        [dq_t[:, h * POS : (h + 1) * POS].T for h in range(HEADS)], axis=1
    ).astype(BF16)
    dkeyval = sum(ref[...].astype(F32) for ref in dkv_refs).astype(BF16)
    grad_ref[...] = (
        dot(dquery, w_query_ref[...], NT) + dot(dkeyval, w_keyval_ref[...], NT)
    ).astype(BF16)
    first = place[0] == 0
    q_low, q_high = dquery[:, :256], dquery[:, 256:]
    kv_low, kv_high = dkeyval[:, :128], dkeyval[:, 128:]
    low = jnp.concatenate([q_low, kv_low], axis=1)
    high = jnp.concatenate([q_high, kv_high], axis=1)
    keep_ref[...] = dot(tokens_ref[...], jnp.where(first, low, high), TN).astype(BF16)
    give_ref[...] = dot(tokens_ref[...], jnp.where(first, high, low), TN).astype(BF16)


VM = pl.BlockSpec(memory_space=pltpu.VMEM)
SM = pl.BlockSpec(memory_space=pltpu.SMEM)


def call(kernel, ins, outs, in_specs, out_specs, scratch, flops):
    return pl.pallas_call(
        kernel,
        out_shape=outs,
        in_specs=in_specs,
        out_specs=out_specs,
        scratch_shapes=scratch,
        compiler_params=pltpu.CompilerParams(vmem_limit_bytes=VMEM_LIMIT),
        cost_estimate=pl.CostEstimate(flops=flops, bytes_accessed=6_000_000, transcendentals=0),
    )(*ins)


def shape(*dims, dtype=BF16):
    return jax.ShapeDtypeStruct(dims, dtype)


def swap(blocks, axes):
    return lax.all_to_all(blocks, axes, 0, 0)


def share(array, axes, count):
    return swap(jnp.broadcast_to(array[None], (count,) + array.shape), axes)


def added(blocks):
    return jnp.sum(blocks.astype(F32), axis=0)


def plus(a, b):
    return (a.astype(F32) + b.astype(F32)).astype(BF16)


def body(tokens, upstream, w_query, w_keyval, w_out):
    local = tokens[0]
    cotangent = upstream[0]
    core = lax.axis_index("core")
    group = lax.axis_index("x") * 2 + lax.axis_index("yl")
    place = jnp.stack([core, group]).astype(jnp.int32)
    query = jnp.dot(local, w_query, preferred_element_type=F32).astype(BF16)
    dmixed = jnp.dot(cotangent, w_out.T, preferred_element_type=F32).astype(BF16)
    qd = jnp.concatenate([query, dmixed], axis=1)
    qds = share(qd, ("x", "yl"), 8)
    qd, early = lax.optimization_barrier((qd, local))
    keyval = jnp.dot(early, w_keyval, preferred_element_type=F32).astype(BF16)
    kvs = [keyval] + [send(keyval, "z", 8, d) for d in range(1, 8)]

    mixed_parts, stats = call(
        forward_kernel,
        [qds, *kvs],
        [shape(8, HEAD_DIM, ROWS), shape(16, ROWS, dtype=F32)],
        [VM] * 9,
        [VM] * 2,
        [
            pltpu.VMEM((KEYS, 2 * HEAD_DIM), BF16),
            pltpu.VMEM((HEAD_DIM, KEYS), BF16),
            pltpu.VMEM((KEYS, ROWS), F32),
        ],
        10_000_000_000,
    )
    all_stats = share(stats, ("x", "yl"), 8)
    mixed_parts, all_stats = lax.optimization_barrier((mixed_parts, all_stats))
    mine = swap(mixed_parts, ("x", "yl"))
    dq_parts, *dkv_parts = call(
        backward_kernel,
        [qds, all_stats, *kvs],
        [shape(8, HEAD_DIM, ROWS)] + [shape(POS, 2 * HEAD_DIM)] * 8,
        [VM] * 10,
        [VM] * 9,
        [
            pltpu.VMEM((KEYS, 2 * HEAD_DIM), BF16),
            pltpu.VMEM((HEAD_DIM, KEYS), BF16),
            pltpu.VMEM((16, ROWS), F32),
            pltpu.VMEM((KEYS, 2 * HEAD_DIM), F32),
        ],
        16_000_000_000,
    )
    dq_parts, mine = lax.optimization_barrier((dq_parts, mine))
    dqs = swap(dq_parts, ("x", "yl"))
    dkvs = [dkv_parts[0]] + [send(dkv_parts[d], "z", 8, -d) for d in range(1, 8)]
    attended, keep_o, give_o = call(
        output_kernel,
        [place, mine, all_stats, local, cotangent, w_out],
        [shape(*local.shape), shape(512, 768), shape(512, 768)],
        [SM] + [VM] * 5,
        [VM] * 3,
        [],
        600_000_000,
    )
    give_o, dqs = lax.optimization_barrier((give_o, dqs))
    got_o = send(give_o, "core", 2, 1)
    term_o = keep_o.astype(F32) + got_o.astype(F32)
    term_o = lax.psum_scatter(term_o, "x", scatter_dimension=0, tiled=True)
    term_o = term_o.reshape(16, 8, 2, 384).transpose(0, 2, 1, 3).reshape(16, 16, 384)

    grad_tokens, keep_i, give_i = call(
        input_kernel,
        [place, dqs, *dkvs, local, w_query, w_keyval],
        [shape(*local.shape), shape(1536, 384), shape(1536, 384)],
        [SM] + [VM] * 12,
        [VM] * 3,
        [],
        900_000_000,
    )
    term_i = plus(keep_i, send(give_i, "core", 2, 1))
    term_i = added(swap(term_i.reshape(4, 384, 384), "x"))
    ends = jnp.concatenate([term_i.reshape(16, 24, 384), term_o], axis=1).astype(BF16)
    ends = added(swap(ends, ("z", "yl")))
    ends = ends + send(ends, "yh", 2, 1)
    other = send(ends, "core", 2, 1)
    low, high = jnp.where(core == 0, ends, other), jnp.where(core == 0, other, ends)
    grad_o = jnp.stack([low[24:], high[24:]]).reshape(2, 2, 8, 384)
    grad_o = grad_o.transpose(2, 0, 1, 3).reshape(8, 1536)
    return (
        attended[None],
        grad_tokens[None],
        jnp.concatenate([low[:24, :256], high[:24, :256]], axis=1),
        jnp.concatenate([low[:24, 256:], high[:24, 256:]], axis=1),
        grad_o,
    )


def solution(mesh):
    torus = Mesh(mesh.devices.reshape(4, 8, 2, 2, 2), AXES)
    return jax.shard_map(
        body,
        mesh=torus,
        in_specs=(P(DP, SEQ, None), P(DP, SEQ, None), P(), P(), P()),
        out_specs=(
            P(DP, SEQ, None),
            P(DP, SEQ, None),
            P(SEQ, None),
            P(SEQ, None),
            P(SEQ, None),
        ),
        check_vma=False,
    )
```

```python
import math

import jax
import jax.numpy as jnp
from jax import lax
from jax.experimental import pallas as pl
from jax.experimental.pallas import tpu as pltpu
from jax.sharding import Mesh, PartitionSpec as P

HEADS = 4
HEAD_DIM = 128
POS = 128
ROWS = HEADS * POS
GROUP = 8
KEYS = 8 * POS
CHUNK = 512
TILE = 32
SCALE = 1.0 / HEAD_DIM**0.5
LOG2E = math.log2(math.e)
AXES = ("x", "z", "yl", "yh", "core")
SEQ = ("x", "z", "yl")
DP = ("yh", "core")
NT = (((1,), (1,)), ((), ()))
TN = (((0,), (0,)), ((), ()))
F32 = jnp.float32
BF16 = jnp.bfloat16
VMEM_LIMIT = 56 * 1024 * 1024


def dot(a, b, dims=(((1,), (0,)), ((), ()))):
    return lax.dot_general(a, b, dims, preferred_element_type=F32)


def send(array, axis, size, step):
    return lax.ppermute(array, axis, [(i, (i + step) % size) for i in range(size)])


def rows_of(block):
    return jnp.concatenate(
        [block[:, h * HEAD_DIM : (h + 1) * HEAD_DIM] for h in range(HEADS)], axis=0
    )


def tiles(count):
    return [slice(t * TILE, (t + 1) * TILE) for t in range(count // TILE)]


def fold(values, op):
    return op(values.reshape(-1, 8, values.shape[1]), axis=0)


def forward_kernel(qd, kv, mixed, stats_ref, vt, *scratch):
    vt[...] = kv[:, HEAD_DIM:].T

    def scores(p, score):
        score[...] = dot(kv[:, :HEAD_DIM], rows_of(qd[p, :, :ROWS]), NT)

    def softmax(p, score, weight):
        top = jnp.full((8, ROWS), -jnp.inf, F32)
        for part in tiles(KEYS):
            top = jnp.maximum(top, fold(score[part, :], jnp.max))
        top = jnp.max(top, axis=0, keepdims=True)
        base = top * (SCALE * LOG2E)
        total = jnp.zeros((8, ROWS), F32)
        for part in tiles(KEYS):
            e = jnp.exp2(score[part, :] * (SCALE * LOG2E) - base)
            total = total + fold(e, jnp.sum)
            weight[part, :] = e.astype(BF16)
        total = jnp.sum(total, axis=0, keepdims=True)
        acc = dot(vt[...], weight[...]) * (1.0 / total)
        mixed[p] = acc.astype(BF16)
        stats_ref[pl.ds(p, 1), :] = top * SCALE + jnp.log(total)
        d4 = rows_of(qd[p, :, ROWS:])
        stats_ref[pl.ds(8 + p, 1), :] = jnp.sum(acc * d4.T.astype(F32), axis=0, keepdims=True)

    def block(i, carry):
        for n in range(2):
            scores(2 * i + n, scratch[n])
        for n in range(2):
            softmax(2 * i + n, scratch[n], scratch[2 + n])
        return carry

    lax.fori_loop(0, GROUP // 2, block, 0)


def combine(logs, bars):
    top = jnp.max(logs, axis=0)
    weights = jnp.exp(logs - top)
    total = jnp.sum(weights, axis=0)
    weights = weights / total
    return top + jnp.log(total), jnp.sum(weights * bars, axis=0), weights


def backward_kernel(qd, stats_ref, kv, dq, dkv_out, kt, stat, dkv, *scratch):
    kt[...] = kv[:, :HEAD_DIM].T
    logsum, delta, unused = combine(stats_ref[:, :8, :], stats_ref[:, 8:, :])
    stat[:8, :] = logsum * LOG2E
    stat[8:, :] = delta
    dkv[...] = jnp.zeros_like(dkv)

    def block(p, carry):
        both = qd[p]
        q4 = rows_of(both[:, :ROWS])
        d4 = rows_of(both[:, ROWS:])
        base = stat[pl.ds(p, 1), :]
        delta = stat[pl.ds(8 + p, 1), :]
        acc = jnp.zeros((HEAD_DIM, ROWS), F32)
        count = KEYS // CHUNK
        for c in range(count):
            part = slice(c * CHUNK, (c + 1) * CHUNK)
            score, dprob = scratch[4 * c : 4 * c + 2]
            score[...] = dot(kv[part, :HEAD_DIM], q4, NT)
            dprob[...] = dot(kv[part, HEAD_DIM:], d4, NT)
        for c in range(count):
            part = slice(c * CHUNK, (c + 1) * CHUNK)
            score, dprob, weight, dscore = scratch[4 * c : 4 * c + 4]
            for tile in tiles(CHUNK):
                prob = jnp.exp2(score[tile, :] * (SCALE * LOG2E) - base)
                weight[tile, :] = prob.astype(BF16)
                dscore[tile, :] = (prob * (dprob[tile, :] - delta)).astype(BF16)
            dkv[part, HEAD_DIM:] += dot(weight[...], d4)
            dkv[part, :HEAD_DIM] += dot(dscore[...], q4)
            acc = acc + dot(kt[:, part], dscore[...])
        dq[p] = (acc * SCALE).astype(BF16)
        return carry

    lax.fori_loop(0, GROUP, block, 0)
    dkv_out[:, :HEAD_DIM] = (dkv[:, :HEAD_DIM] * SCALE).astype(BF16)
    dkv_out[:, HEAD_DIM:] = dkv[:, HEAD_DIM:].astype(BF16)


def output_kernel(place, parts, stats_ref, tokens_ref, upstream_ref, w_out_ref, *outs):
    attended_ref, keep_ref, give_ref = outs
    mine = place[1]
    unused, unused, weights = combine(
        stats_ref[:, pl.ds(mine, 1), :], stats_ref[:, pl.ds(8 + mine, 1), :]
    )
    mixed_t = jnp.sum(weights * parts[...].astype(F32), axis=0)
    heads_t = [mixed_t[:, h * POS : (h + 1) * POS] for h in range(HEADS)]
    mixed = jnp.concatenate([m.T for m in heads_t], axis=1).astype(BF16)
    mixed_rows = jnp.concatenate(heads_t, axis=0).astype(BF16)
    attended_ref[...] = (
        tokens_ref[...].astype(F32) + dot(mixed, w_out_ref[...])
    ).astype(BF16)
    half = upstream_ref.shape[1] // 2
    first = place[0] == 0
    low, high = upstream_ref[:, :half], upstream_ref[:, half:]
    keep_ref[...] = dot(mixed_rows, jnp.where(first, low, high)).astype(BF16)
    give_ref[...] = dot(mixed_rows, jnp.where(first, high, low)).astype(BF16)


def input_kernel(place, dq_ref, dkv_ref, tokens_ref, w_query_ref, w_keyval_ref, *outs):
    grad_ref, keep_ref, give_ref = outs
    dq_t = jnp.sum(dq_ref[...].astype(F32), axis=0)
    dquery = jnp.concatenate(
        [dq_t[:, h * POS : (h + 1) * POS].T for h in range(HEADS)], axis=1
    ).astype(BF16)
    dkeyval = jnp.sum(dkv_ref[...].astype(F32), axis=0).astype(BF16)
    grad_ref[...] = (
        dot(dquery, w_query_ref[...], NT) + dot(dkeyval, w_keyval_ref[...], NT)
    ).astype(BF16)
    first = place[0] == 0
    q_low, q_high = dquery[:, :256], dquery[:, 256:]
    kv_low, kv_high = dkeyval[:, :128], dkeyval[:, 128:]
    low = jnp.concatenate([q_low, kv_low], axis=1)
    high = jnp.concatenate([q_high, kv_high], axis=1)
    keep_ref[...] = dot(tokens_ref[...], jnp.where(first, low, high), TN).astype(BF16)
    give_ref[...] = dot(tokens_ref[...], jnp.where(first, high, low), TN).astype(BF16)


VM = pl.BlockSpec(memory_space=pltpu.VMEM)
SM = pl.BlockSpec(memory_space=pltpu.SMEM)


def call(kernel, ins, outs, in_specs, out_specs, scratch, flops):
    return pl.pallas_call(
        kernel,
        out_shape=outs,
        in_specs=in_specs,
        out_specs=out_specs,
        scratch_shapes=scratch,
        compiler_params=pltpu.CompilerParams(vmem_limit_bytes=VMEM_LIMIT),
        cost_estimate=pl.CostEstimate(flops=flops, bytes_accessed=6_000_000, transcendentals=0),
    )(*ins)


def shape(*dims, dtype=BF16):
    return jax.ShapeDtypeStruct(dims, dtype)


def swap(blocks, axes):
    return lax.all_to_all(blocks, axes, 0, 0)


def share(array, axes, count):
    return swap(jnp.broadcast_to(array[None], (count,) + array.shape), axes)


def added(blocks):
    return jnp.sum(blocks.astype(F32), axis=0)


def plus(a, b):
    return (a.astype(F32) + b.astype(F32)).astype(BF16)


def body(tokens, upstream, w_query, w_keyval, w_out):
    local = tokens[0]
    cotangent = upstream[0]
    core = lax.axis_index("core")
    group = lax.axis_index("x") * 2 + lax.axis_index("yl")
    place = jnp.stack([core, group]).astype(jnp.int32)
    query = jnp.dot(local, w_query, preferred_element_type=F32).astype(BF16)
    dmixed = jnp.dot(cotangent, w_out.T, preferred_element_type=F32).astype(BF16)
    qd = jnp.concatenate([query, dmixed], axis=1)
    qds = share(qd, ("x", "yl"), 8)
    qd, early = lax.optimization_barrier((qd, local))
    keyval = jnp.dot(early, w_keyval, preferred_element_type=F32).astype(BF16)
    kvs = lax.all_gather(keyval, "z", axis=0, tiled=True)

    mixed_parts, stats = call(
        forward_kernel,
        [qds, kvs],
        [shape(8, HEAD_DIM, ROWS), shape(16, ROWS, dtype=F32)],
        [VM] * 2,
        [VM] * 2,
        [
            pltpu.VMEM((HEAD_DIM, KEYS), BF16),
            pltpu.VMEM((KEYS, ROWS), F32),
            pltpu.VMEM((KEYS, ROWS), F32),
            pltpu.VMEM((KEYS, ROWS), BF16),
            pltpu.VMEM((KEYS, ROWS), BF16),
        ],
        10_000_000_000,
    )
    all_stats = share(stats, ("x", "yl"), 8)
    mixed_parts, all_stats = lax.optimization_barrier((mixed_parts, all_stats))
    mine = swap(mixed_parts, ("x", "yl"))
    dq_parts, dkv_parts = call(
        backward_kernel,
        [qds, all_stats, kvs],
        [shape(8, HEAD_DIM, ROWS), shape(KEYS, 2 * HEAD_DIM)],
        [VM] * 3,
        [VM] * 2,
        [
            pltpu.VMEM((HEAD_DIM, KEYS), BF16),
            pltpu.VMEM((16, ROWS), F32),
            pltpu.VMEM((KEYS, 2 * HEAD_DIM), F32),
        ]
        + [pltpu.VMEM((CHUNK, ROWS), t) for t in (F32, F32, BF16, BF16)] * (KEYS // CHUNK),
        16_000_000_000,
    )
    dq_parts, dkv_parts, mine = lax.optimization_barrier((dq_parts, dkv_parts, mine))
    dkv = swap(dkv_parts.reshape(8, POS, 2 * HEAD_DIM), "z")
    attended, keep_o, give_o = call(
        output_kernel,
        [place, mine, all_stats, local, cotangent, w_out],
        [shape(*local.shape), shape(512, 768), shape(512, 768)],
        [SM] + [VM] * 5,
        [VM] * 3,
        [],
        600_000_000,
    )
    give_o, dkv, dq_parts = lax.optimization_barrier((give_o, dkv, dq_parts))
    term_o = keep_o.astype(F32) + send(give_o, "core", 2, 1).astype(F32)
    dqs = swap(dq_parts, ("x", "yl"))
    unused, dqs = lax.optimization_barrier((term_o, dqs))
    term_o = term_o.reshape(32, 2, 8, 2, 384).transpose(3, 1, 0, 2, 4).reshape(1024, 384)
    term_o = lax.psum_scatter(term_o, ("yh", "yl"), scatter_dimension=0, tiled=True)

    grad_tokens, keep_i, give_i = call(
        input_kernel,
        [place, dqs, dkv, local, w_query, w_keyval],
        [shape(*local.shape), shape(1536, 384), shape(1536, 384)],
        [SM] + [VM] * 5,
        [VM] * 3,
        [],
        900_000_000,
    )
    term_i = plus(keep_i, send(give_i, "core", 2, 1)).reshape(4, 384, 384)
    terms = jnp.concatenate([term_i, term_o.astype(BF16).reshape(4, 64, 384)], axis=1)
    terms = added(swap(terms, "x"))
    term_i = terms[:384].reshape(8, 2, 24, 384)
    here = (jnp.arange(2) == lax.axis_index("yl"))[None, :, None, None]
    term_o = jnp.where(here, terms[384:].reshape(8, 1, 8, 384), 0.0)
    ends = jnp.concatenate([term_i, term_o], axis=2).astype(BF16).reshape(16, 32, 384)
    ends = added(swap(ends, ("z", "yl")))
    got = send(ends, "yh", 2, 1)
    yh = lax.axis_index("yh")
    ends = jnp.concatenate(
        [
            ends[:24] + got[:24],
            jnp.where(yh == 0, ends[24:], got[24:]),
            jnp.where(yh == 0, got[24:], ends[24:]),
        ]
    )
    other = send(ends, "core", 2, 1)
    low, high = jnp.where(core == 0, ends, other), jnp.where(core == 0, other, ends)
    grad_o = jnp.concatenate([low[24:32], low[32:], high[24:32], high[32:]], axis=1)
    return (
        attended[None],
        grad_tokens[None],
        jnp.concatenate([low[:24, :256], high[:24, :256]], axis=1),
        jnp.concatenate([low[:24, 256:], high[:24, 256:]], axis=1),
        grad_o,
    )


def solution(mesh):
    torus = Mesh(mesh.devices.reshape(4, 8, 2, 2, 2), AXES)
    return jax.shard_map(
        body,
        mesh=torus,
        in_specs=(P(DP, SEQ, None), P(DP, SEQ, None), P(), P(), P()),
        out_specs=(
            P(DP, SEQ, None),
            P(DP, SEQ, None),
            P(SEQ, None),
            P(SEQ, None),
            P(SEQ, None),
        ),
        check_vma=False,
    )
```

```python
import math

import jax
import jax.numpy as jnp
from jax import lax
from jax.experimental import pallas as pl
from jax.experimental.pallas import tpu as pltpu
from jax.sharding import Mesh, PartitionSpec as P

HEADS = 4
HEAD_DIM = 128
POS = 128
ROWS = HEADS * POS
GROUP = 8
KEYS = 8 * POS
CHUNK = 512
TILE = 32
SCALE = 1.0 / HEAD_DIM**0.5
LOG2E = math.log2(math.e)
AXES = ("x", "z", "yl", "yh", "core")
SEQ = ("x", "z", "yl")
DP = ("yh", "core")
NT = (((1,), (1,)), ((), ()))
TN = (((0,), (0,)), ((), ()))
F32 = jnp.float32
BF16 = jnp.bfloat16
VMEM_LIMIT = 56 * 1024 * 1024


def dot(a, b, dims=(((1,), (0,)), ((), ()))):
    return lax.dot_general(a, b, dims, preferred_element_type=F32)


def send(array, axis, size, step):
    return lax.ppermute(array, axis, [(i, (i + step) % size) for i in range(size)])


def rows_of(block):
    return jnp.concatenate(
        [block[:, h * HEAD_DIM : (h + 1) * HEAD_DIM] for h in range(HEADS)], axis=0
    )


def tiles(count):
    return [slice(t * TILE, (t + 1) * TILE) for t in range(count // TILE)]


def fold(values, op):
    return op(values.reshape(-1, 8, values.shape[1]), axis=0)


def forward_kernel(qd, kv, mixed, stats_ref, vt, *scratch):
    vt[...] = kv[:, HEAD_DIM:].T

    def scores(p, score):
        score[...] = dot(kv[:, :HEAD_DIM], rows_of(qd[p, :, :ROWS]), NT)

    def softmax(p, score, weight):
        top = jnp.full((8, ROWS), -jnp.inf, F32)
        for part in tiles(KEYS):
            top = jnp.maximum(top, fold(score[part, :], jnp.max))
        top = jnp.max(top, axis=0, keepdims=True)
        base = top * (SCALE * LOG2E)
        total = jnp.zeros((8, ROWS), F32)
        for part in tiles(KEYS):
            e = jnp.exp2(score[part, :] * (SCALE * LOG2E) - base)
            total = total + fold(e, jnp.sum)
            weight[part, :] = e.astype(BF16)
        total = jnp.sum(total, axis=0, keepdims=True)
        acc = dot(vt[...], weight[...]) * (1.0 / total)
        mixed[p] = acc.astype(BF16)
        stats_ref[pl.ds(p, 1), :] = top * SCALE + jnp.log(total)
        d4 = rows_of(qd[p, :, ROWS:])
        stats_ref[pl.ds(8 + p, 1), :] = jnp.sum(acc * d4.T.astype(F32), axis=0, keepdims=True)

    def block(i, carry):
        for n in range(2):
            scores(2 * i + n, scratch[n])
        for n in range(2):
            softmax(2 * i + n, scratch[n], scratch[2 + n])
        return carry

    lax.fori_loop(0, GROUP // 2, block, 0)


def combine(logs, bars):
    top = jnp.max(logs, axis=0)
    weights = jnp.exp(logs - top)
    total = jnp.sum(weights, axis=0)
    weights = weights / total
    return top + jnp.log(total), jnp.sum(weights * bars, axis=0), weights


def backward_kernel(qd, stats_ref, kv, dq, dkv, kt, stat, *scratch):
    kt[...] = kv[:, :HEAD_DIM].T
    logsum, delta, unused = combine(stats_ref[:, :8, :], stats_ref[:, 8:, :])
    stat[:8, :] = logsum * LOG2E
    stat[8:, :] = delta
    dkv[...] = jnp.zeros_like(dkv)

    def block(p, carry):
        both = qd[p]
        q4 = rows_of(both[:, :ROWS])
        d4 = rows_of(both[:, ROWS:])
        base = stat[pl.ds(p, 1), :]
        delta = stat[pl.ds(8 + p, 1), :]
        acc = jnp.zeros((HEAD_DIM, ROWS), F32)
        count = KEYS // CHUNK
        for c in range(count):
            part = slice(c * CHUNK, (c + 1) * CHUNK)
            score, dprob = scratch[4 * c : 4 * c + 2]
            score[...] = dot(kv[part, :HEAD_DIM], q4, NT)
            dprob[...] = dot(kv[part, HEAD_DIM:], d4, NT)
        for c in range(count):
            part = slice(c * CHUNK, (c + 1) * CHUNK)
            score, dprob, weight, dscore = scratch[4 * c : 4 * c + 4]
            for tile in tiles(CHUNK):
                prob = jnp.exp2(score[tile, :] * (SCALE * LOG2E) - base)
                weight[tile, :] = prob.astype(BF16)
                dscore[tile, :] = (prob * (dprob[tile, :] - delta)).astype(BF16)
            dkv[part, HEAD_DIM:] += dot(weight[...], d4)
            dkv[part, :HEAD_DIM] += dot(dscore[...], q4)
            acc = acc + dot(kt[:, part], dscore[...])
        dq[p] = (acc * SCALE).astype(BF16)
        return carry

    lax.fori_loop(0, GROUP, block, 0)
    dkv[:, :HEAD_DIM] = dkv[:, :HEAD_DIM] * SCALE


def output_kernel(place, parts, stats_ref, tokens_ref, upstream_ref, w_out_ref, *outs):
    attended_ref, keep_ref, give_ref = outs
    mine = place[1]
    unused, unused, weights = combine(
        stats_ref[:, pl.ds(mine, 1), :], stats_ref[:, pl.ds(8 + mine, 1), :]
    )
    mixed_t = jnp.sum(weights * parts[...].astype(F32), axis=0)
    heads_t = [mixed_t[:, h * POS : (h + 1) * POS] for h in range(HEADS)]
    mixed = jnp.concatenate([m.T for m in heads_t], axis=1).astype(BF16)
    mixed_rows = jnp.concatenate(heads_t, axis=0).astype(BF16)
    attended_ref[...] = (
        tokens_ref[...].astype(F32) + dot(mixed, w_out_ref[...])
    ).astype(BF16)
    half = upstream_ref.shape[1] // 2
    first = place[0] == 0
    low, high = upstream_ref[:, :half], upstream_ref[:, half:]
    keep_ref[...] = dot(mixed_rows, jnp.where(first, low, high)).astype(BF16)
    give_ref[...] = dot(mixed_rows, jnp.where(first, high, low)).astype(BF16)


def input_kernel(place, dq_ref, dkv_ref, tokens_ref, both_ref, keep_ref, give_ref):
    dq_t = jnp.sum(dq_ref[...].astype(F32), axis=0)
    dquery = jnp.concatenate(
        [dq_t[:, h * POS : (h + 1) * POS].T for h in range(HEADS)], axis=1
    ).astype(BF16)
    dkeyval = dkv_ref[...].astype(BF16)
    both_ref[:, :ROWS] = dquery
    both_ref[:, ROWS:] = dkeyval
    first = place[0] == 0
    q_low, q_high = dquery[:, :256], dquery[:, 256:]
    kv_low, kv_high = dkeyval[:, :128], dkeyval[:, 128:]
    low = jnp.concatenate([q_low, kv_low], axis=1)
    high = jnp.concatenate([q_high, kv_high], axis=1)
    keep_ref[...] = dot(tokens_ref[...], jnp.where(first, low, high), TN).astype(BF16)
    give_ref[...] = dot(tokens_ref[...], jnp.where(first, high, low), TN).astype(BF16)


def tokens_kernel(both_ref, w_query_ref, w_keyval_ref, grad_ref):
    grad_ref[...] = (
        dot(both_ref[:, :ROWS], w_query_ref[...], NT)
        + dot(both_ref[:, ROWS:], w_keyval_ref[...], NT)
    ).astype(BF16)


def plus(a, b):
    return (a.astype(F32) + b.astype(F32)).astype(BF16)


VM = pl.BlockSpec(memory_space=pltpu.VMEM)
SM = pl.BlockSpec(memory_space=pltpu.SMEM)


def call(kernel, ins, outs, in_specs, out_specs, scratch, flops):
    return pl.pallas_call(
        kernel,
        out_shape=outs,
        in_specs=in_specs,
        out_specs=out_specs,
        scratch_shapes=scratch,
        compiler_params=pltpu.CompilerParams(vmem_limit_bytes=VMEM_LIMIT),
        cost_estimate=pl.CostEstimate(flops=flops, bytes_accessed=6_000_000, transcendentals=0),
    )(*ins)


def shape(*dims, dtype=BF16):
    return jax.ShapeDtypeStruct(dims, dtype)


def swap(blocks, axes):
    return lax.all_to_all(blocks, axes, 0, 0)


def share(array, axes, count):
    return swap(jnp.broadcast_to(array[None], (count,) + array.shape), axes)


def added(blocks):
    return jnp.sum(blocks.astype(F32), axis=0)


def body(tokens, upstream, w_query, w_keyval, w_out):
    local = tokens[0]
    cotangent = upstream[0]
    core = lax.axis_index("core")
    group = lax.axis_index("x") * 2 + lax.axis_index("yl")
    place = jnp.stack([core, group]).astype(jnp.int32)
    query = jnp.dot(local, w_query, preferred_element_type=F32).astype(BF16)
    dmixed = jnp.dot(cotangent, w_out.T, preferred_element_type=F32).astype(BF16)
    qd = jnp.concatenate([query, dmixed], axis=1)
    qds = share(qd, ("x", "yl"), 8)
    qd, early = lax.optimization_barrier((qd, local))
    keyval = jnp.dot(early, w_keyval, preferred_element_type=F32).astype(BF16)
    kvs = lax.all_gather(keyval, "z", axis=0, tiled=True)

    mixed_parts, stats = call(
        forward_kernel,
        [qds, kvs],
        [shape(8, HEAD_DIM, ROWS), shape(16, ROWS, dtype=F32)],
        [VM] * 2,
        [VM] * 2,
        [
            pltpu.VMEM((HEAD_DIM, KEYS), BF16),
            pltpu.VMEM((KEYS, ROWS), F32),
            pltpu.VMEM((KEYS, ROWS), F32),
            pltpu.VMEM((KEYS, ROWS), BF16),
            pltpu.VMEM((KEYS, ROWS), BF16),
        ],
        10_000_000_000,
    )
    all_stats = share(stats, ("x", "yl"), 8)
    mixed_parts, all_stats = lax.optimization_barrier((mixed_parts, all_stats))
    mine = swap(mixed_parts, ("x", "yl"))
    dq_parts, dkv_parts = call(
        backward_kernel,
        [qds, all_stats, kvs],
        [shape(8, HEAD_DIM, ROWS), shape(KEYS, 2 * HEAD_DIM, dtype=F32)],
        [VM] * 3,
        [VM] * 2,
        [
            pltpu.VMEM((HEAD_DIM, KEYS), BF16),
            pltpu.VMEM((16, ROWS), F32),
        ]
        + [pltpu.VMEM((CHUNK, ROWS), t) for t in (F32, F32, BF16, BF16)] * (KEYS // CHUNK),
        16_000_000_000,
    )
    dq_parts, mine = lax.optimization_barrier((dq_parts, mine))
    dkv = lax.psum_scatter(dkv_parts, "z", scatter_dimension=0, tiled=True)
    attended, keep_o, give_o = call(
        output_kernel,
        [place, mine, all_stats, local, cotangent, w_out],
        [shape(*local.shape), shape(512, 768), shape(512, 768)],
        [SM] + [VM] * 5,
        [VM] * 3,
        [],
        600_000_000,
    )
    term_o = plus(keep_o, send(give_o, "core", 2, 1))
    term_o, dq_parts = lax.optimization_barrier((term_o, dq_parts))
    dqs = swap(dq_parts, ("x", "yl"))
    term_o = added(swap(term_o.reshape(4, 128, 768), "x"))
    term_o = term_o.reshape(16, 8, 2, 384).transpose(0, 2, 1, 3).reshape(16, 16, 384)
    dkv, term_o = lax.optimization_barrier((dkv, term_o))

    both, keep_i, give_i = call(
        input_kernel,
        [place, dqs, dkv, local],
        [shape(POS, 768), shape(1536, 384), shape(1536, 384)],
        [SM] + [VM] * 3,
        [VM] * 3,
        [],
        600_000_000,
    )
    term_i = plus(keep_i, send(give_i, "core", 2, 1))
    grad_tokens = call(
        tokens_kernel,
        [both, w_query, w_keyval],
        shape(*local.shape),
        [VM] * 3,
        VM,
        [],
        300_000_000,
    )
    term_i = swap(term_i.reshape(4, 384, 384), "x")
    grad_tokens, term_i = lax.optimization_barrier((grad_tokens, term_i))
    term_i = added(term_i)
    ends = jnp.concatenate([term_i.reshape(16, 24, 384), term_o], axis=1).astype(BF16)
    ends = added(swap(ends, ("z", "yl")))
    ends = ends + send(ends, "yh", 2, 1)
    other = send(ends, "core", 2, 1)
    low, high = jnp.where(core == 0, ends, other), jnp.where(core == 0, other, ends)
    grad_o = jnp.stack([low[24:], high[24:]]).reshape(2, 2, 8, 384)
    grad_o = grad_o.transpose(2, 0, 1, 3).reshape(8, 1536)
    return (
        attended[None],
        grad_tokens[None],
        jnp.concatenate([low[:24, :256], high[:24, :256]], axis=1),
        jnp.concatenate([low[:24, 256:], high[:24, 256:]], axis=1),
        grad_o,
    )


def solution(mesh):
    torus = Mesh(mesh.devices.reshape(4, 8, 2, 2, 2), AXES)
    return jax.shard_map(
        body,
        mesh=torus,
        in_specs=(P(DP, SEQ, None), P(DP, SEQ, None), P(), P(), P()),
        out_specs=(
            P(DP, SEQ, None),
            P(DP, SEQ, None),
            P(SEQ, None),
            P(SEQ, None),
            P(SEQ, None),
        ),
        check_vma=False,
    )
```

```python
import math

import jax
import jax.numpy as jnp
from jax import lax
from jax.experimental import pallas as pl
from jax.experimental.pallas import tpu as pltpu
from jax.sharding import Mesh, PartitionSpec as P

HEADS = 4
HEAD_DIM = 128
POS = 128
ROWS = HEADS * POS
GROUP = 8
KEYS = 8 * POS
TILE = 32
SCALE = 1.0 / HEAD_DIM**0.5
LOG2E = math.log2(math.e)
AXES = ("x", "z", "yl", "yh", "core")
SEQ = ("x", "z", "yl")
DP = ("yh", "core")
NT = (((1,), (1,)), ((), ()))
TN = (((0,), (0,)), ((), ()))
F32 = jnp.float32
BF16 = jnp.bfloat16
VMEM_LIMIT = 56 * 1024 * 1024


def dot(a, b, dims=(((1,), (0,)), ((), ()))):
    return lax.dot_general(a, b, dims, preferred_element_type=F32)


def send(array, axis, size, step):
    return lax.ppermute(array, axis, [(i, (i + step) % size) for i in range(size)])


def rows_of(block):
    return jnp.concatenate(
        [block[:, h * HEAD_DIM : (h + 1) * HEAD_DIM] for h in range(HEADS)], axis=0
    )


def tiles(count):
    return [slice(t * TILE, (t + 1) * TILE) for t in range(count // TILE)]


def fold(values, op):
    return op(values.reshape(-1, 8, values.shape[1]), axis=0)


def forward_kernel(qd, kv, mixed, stats_ref, vt, *scratch):
    vt[...] = kv[:, HEAD_DIM:].T

    def scores(p, score):
        score[...] = dot(kv[:, :HEAD_DIM], rows_of(qd[p, :, :ROWS]), NT)

    def softmax(p, score, weight):
        top = jnp.full((8, ROWS), -jnp.inf, F32)
        for part in tiles(KEYS):
            top = jnp.maximum(top, fold(score[part, :], jnp.max))
        top = jnp.max(top, axis=0, keepdims=True)
        base = top * (SCALE * LOG2E)
        total = jnp.zeros((8, ROWS), F32)
        for part in tiles(KEYS):
            e = jnp.exp2(score[part, :] * (SCALE * LOG2E) - base)
            total = total + fold(e, jnp.sum)
            weight[part, :] = e.astype(BF16)
        total = jnp.sum(total, axis=0, keepdims=True)
        acc = dot(vt[...], weight[...]) * (1.0 / total)
        mixed[p] = acc.astype(BF16)
        stats_ref[pl.ds(p, 1), :] = top * SCALE + jnp.log(total)
        d4 = rows_of(qd[p, :, ROWS:])
        stats_ref[pl.ds(8 + p, 1), :] = jnp.sum(acc * d4.T.astype(F32), axis=0, keepdims=True)

    def block(i, carry):
        for n in range(2):
            scores(2 * i + n, scratch[n])
        for n in range(2):
            softmax(2 * i + n, scratch[n], scratch[2 + n])
        return carry

    lax.fori_loop(0, GROUP // 2, block, 0)


def combine(logs, bars):
    top = jnp.max(logs, axis=0)
    weights = jnp.exp(logs - top)
    total = jnp.sum(weights, axis=0)
    weights = weights / total
    return top + jnp.log(total), jnp.sum(weights * bars, axis=0), weights


def backward_kernel(qd, stats_ref, kv, dq, dkv, kt, stat, *scratch):
    kt[...] = kv[:, :HEAD_DIM].T
    logsum, delta, unused = combine(stats_ref[:, :8, :], stats_ref[:, 8:, :])
    stat[:8, :] = logsum * LOG2E
    stat[8:, :] = delta
    dkv[...] = jnp.zeros_like(dkv)

    def rows(p):
        return rows_of(qd[p, :, :ROWS]), rows_of(qd[p, :, ROWS:])

    def products(p, score, dprob):
        q4, d4 = rows(p)
        score[...] = dot(kv[:, :HEAD_DIM], q4, NT)
        dprob[...] = dot(kv[:, HEAD_DIM:], d4, NT)

    def gradients(p, score, dprob, weight, dscore):
        base = stat[pl.ds(p, 1), :]
        delta = stat[pl.ds(8 + p, 1), :]
        for tile in tiles(KEYS):
            prob = jnp.exp2(score[tile, :] * (SCALE * LOG2E) - base)
            weight[tile, :] = prob.astype(BF16)
            dscore[tile, :] = (prob * (dprob[tile, :] - delta)).astype(BF16)
        q4, d4 = rows(p)
        dkv[:, HEAD_DIM:] += dot(weight[...], d4)
        dkv[:, :HEAD_DIM] += dot(dscore[...], q4)
        dq[p] = (dot(kt[...], dscore[...]) * SCALE).astype(BF16)

    def block(i, carry):
        for n in range(2):
            products(2 * i + n, *scratch[4 * n : 4 * n + 2])
        for n in range(2):
            gradients(2 * i + n, *scratch[4 * n : 4 * n + 4])
        return carry

    lax.fori_loop(0, GROUP // 2, block, 0)
    dkv[:, :HEAD_DIM] = dkv[:, :HEAD_DIM] * SCALE


def output_kernel(place, parts, stats_ref, upstream_ref, mixed_ref, keep_ref, give_ref):
    mine = place[1]
    unused, unused, weights = combine(
        stats_ref[:, pl.ds(mine, 1), :], stats_ref[:, pl.ds(8 + mine, 1), :]
    )
    mixed_t = jnp.sum(weights * parts[...].astype(F32), axis=0)
    heads_t = [mixed_t[:, h * POS : (h + 1) * POS] for h in range(HEADS)]
    mixed_ref[...] = jnp.concatenate([m.T for m in heads_t], axis=1).astype(BF16)
    mixed_rows = jnp.concatenate(heads_t, axis=0).astype(BF16)
    half = upstream_ref.shape[1] // 2
    first = place[0] == 0
    low, high = upstream_ref[:, :half], upstream_ref[:, half:]
    keep_ref[...] = dot(mixed_rows, jnp.where(first, low, high)).astype(BF16)
    give_ref[...] = dot(mixed_rows, jnp.where(first, high, low)).astype(BF16)


def attended_kernel(tokens_ref, mixed_ref, w_out_ref, attended_ref):
    attended_ref[...] = (
        tokens_ref[...].astype(F32) + dot(mixed_ref[...], w_out_ref[...])
    ).astype(BF16)


def input_kernel(place, dq_ref, dkv_ref, tokens_ref, both_ref, keep_ref, give_ref):
    dq_t = jnp.sum(dq_ref[...].astype(F32), axis=0)
    dquery = jnp.concatenate(
        [dq_t[:, h * POS : (h + 1) * POS].T for h in range(HEADS)], axis=1
    ).astype(BF16)
    dkeyval = dkv_ref[...].astype(BF16)
    both_ref[:, :ROWS] = dquery
    both_ref[:, ROWS:] = dkeyval
    first = place[0] == 0
    q_low, q_high = dquery[:, :256], dquery[:, 256:]
    kv_low, kv_high = dkeyval[:, :128], dkeyval[:, 128:]
    low = jnp.concatenate([q_low, kv_low], axis=1)
    high = jnp.concatenate([q_high, kv_high], axis=1)
    keep_ref[...] = dot(tokens_ref[...], jnp.where(first, low, high), TN).astype(BF16)
    give_ref[...] = dot(tokens_ref[...], jnp.where(first, high, low), TN).astype(BF16)


def tokens_kernel(both_ref, w_query_ref, w_keyval_ref, grad_ref):
    grad_ref[...] = (
        dot(both_ref[:, :ROWS], w_query_ref[...], NT)
        + dot(both_ref[:, ROWS:], w_keyval_ref[...], NT)
    ).astype(BF16)


def plus(a, b):
    return (a.astype(F32) + b.astype(F32)).astype(BF16)


VM = pl.BlockSpec(memory_space=pltpu.VMEM)
SM = pl.BlockSpec(memory_space=pltpu.SMEM)


def call(kernel, ins, outs, in_specs, out_specs, scratch, flops):
    return pl.pallas_call(
        kernel,
        out_shape=outs,
        in_specs=in_specs,
        out_specs=out_specs,
        scratch_shapes=scratch,
        compiler_params=pltpu.CompilerParams(vmem_limit_bytes=VMEM_LIMIT),
        cost_estimate=pl.CostEstimate(flops=flops, bytes_accessed=6_000_000, transcendentals=0),
    )(*ins)


def shape(*dims, dtype=BF16):
    return jax.ShapeDtypeStruct(dims, dtype)


def swap(blocks, axes):
    return lax.all_to_all(blocks, axes, 0, 0)


def share(array, axes, count):
    return swap(jnp.broadcast_to(array[None], (count,) + array.shape), axes)


def added(blocks):
    return jnp.sum(blocks.astype(F32), axis=0)


def body(tokens, upstream, w_query, w_keyval, w_out):
    local = tokens[0]
    cotangent = upstream[0]
    core = lax.axis_index("core")
    group = lax.axis_index("x") * 2 + lax.axis_index("yl")
    place = jnp.stack([core, group]).astype(jnp.int32)
    query = jnp.dot(local, w_query, preferred_element_type=F32).astype(BF16)
    dmixed = jnp.dot(cotangent, w_out.T, preferred_element_type=F32).astype(BF16)
    qd = jnp.concatenate([query, dmixed], axis=1)
    qds = share(qd, ("x", "yl"), 8)
    qd, early = lax.optimization_barrier((qd, local))
    keyval = jnp.dot(early, w_keyval, preferred_element_type=F32).astype(BF16)
    kvs = lax.all_gather(keyval, "z", axis=0, tiled=True)

    mixed_parts, stats = call(
        forward_kernel,
        [qds, kvs],
        [shape(8, HEAD_DIM, ROWS), shape(16, ROWS, dtype=F32)],
        [VM] * 2,
        [VM] * 2,
        [
            pltpu.VMEM((HEAD_DIM, KEYS), BF16),
            pltpu.VMEM((KEYS, ROWS), F32),
            pltpu.VMEM((KEYS, ROWS), F32),
            pltpu.VMEM((KEYS, ROWS), BF16),
            pltpu.VMEM((KEYS, ROWS), BF16),
        ],
        10_000_000_000,
    )
    all_stats = share(stats, ("x", "yl"), 8)
    mixed_parts, all_stats = lax.optimization_barrier((mixed_parts, all_stats))
    mine = swap(mixed_parts, ("x", "yl"))
    dq_parts, dkv_parts = call(
        backward_kernel,
        [qds, all_stats, kvs],
        [shape(8, HEAD_DIM, ROWS), shape(KEYS, 2 * HEAD_DIM, dtype=F32)],
        [VM] * 3,
        [VM] * 2,
        [
            pltpu.VMEM((HEAD_DIM, KEYS), BF16),
            pltpu.VMEM((16, ROWS), F32),
        ]
        + [pltpu.VMEM((KEYS, ROWS), t) for t in (F32, F32, BF16, BF16)] * 2,
        16_000_000_000,
    )
    dq_parts, mine = lax.optimization_barrier((dq_parts, mine))
    dkv = lax.psum_scatter(dkv_parts, "z", scatter_dimension=0, tiled=True)
    mixed, keep_o, give_o = call(
        output_kernel,
        [place, mine, all_stats, cotangent],
        [shape(POS, ROWS), shape(512, 768), shape(512, 768)],
        [SM] + [VM] * 3,
        [VM] * 3,
        [],
        400_000_000,
    )
    term_o = plus(keep_o, send(give_o, "core", 2, 1))
    dqs = swap(dq_parts, ("x", "yl"))
    term_o, dqs = lax.optimization_barrier((term_o, dqs))
    term_o = added(swap(term_o.reshape(4, 128, 768), "x"))
    term_o = term_o.reshape(16, 8, 2, 384).transpose(0, 2, 1, 3).reshape(16, 16, 384)
    dkv, term_o = lax.optimization_barrier((dkv, term_o))

    both, keep_i, give_i = call(
        input_kernel,
        [place, dqs, dkv, local],
        [shape(POS, 768), shape(1536, 384), shape(1536, 384)],
        [SM] + [VM] * 3,
        [VM] * 3,
        [],
        600_000_000,
    )
    term_i = plus(keep_i, send(give_i, "core", 2, 1))
    grad_tokens = call(
        tokens_kernel,
        [both, w_query, w_keyval],
        shape(*local.shape),
        [VM] * 3,
        VM,
        [],
        300_000_000,
    )
    term_i = swap(term_i.reshape(4, 384, 384), "x")
    grad_tokens, term_i = lax.optimization_barrier((grad_tokens, term_i))
    term_i = added(term_i)
    ends = jnp.concatenate([term_i.reshape(16, 24, 384), term_o], axis=1).astype(BF16)
    attended = call(
        attended_kernel,
        [local, mixed, w_out],
        shape(*local.shape),
        [VM] * 3,
        VM,
        [],
        200_000_000,
    )
    ends = swap(ends, ("z", "yl"))
    attended, ends = lax.optimization_barrier((attended, ends))
    ends = added(ends)
    ends = ends + send(ends, "yh", 2, 1)
    other = send(ends, "core", 2, 1)
    low, high = jnp.where(core == 0, ends, other), jnp.where(core == 0, other, ends)
    grad_o = jnp.stack([low[24:], high[24:]]).reshape(2, 2, 8, 384)
    grad_o = grad_o.transpose(2, 0, 1, 3).reshape(8, 1536)
    return (
        attended[None],
        grad_tokens[None],
        jnp.concatenate([low[:24, :256], high[:24, :256]], axis=1),
        jnp.concatenate([low[:24, 256:], high[:24, 256:]], axis=1),
        grad_o,
    )


def solution(mesh):
    torus = Mesh(mesh.devices.reshape(4, 8, 2, 2, 2), AXES)
    return jax.shard_map(
        body,
        mesh=torus,
        in_specs=(P(DP, SEQ, None), P(DP, SEQ, None), P(), P(), P()),
        out_specs=(
            P(DP, SEQ, None),
            P(DP, SEQ, None),
            P(SEQ, None),
            P(SEQ, None),
            P(SEQ, None),
        ),
        check_vma=False,
    )
```

```python
import math

import jax
import jax.numpy as jnp
from jax import lax
from jax.experimental import pallas as pl
from jax.experimental.pallas import tpu as pltpu
from jax.sharding import Mesh, PartitionSpec as P

HEADS = 4
HEAD_DIM = 128
POS = 128
ROWS = HEADS * POS
GROUP = 8
KEYS = 8 * POS
TILE = 32
SCALE = 1.0 / HEAD_DIM**0.5
LOG2E = math.log2(math.e)
AXES = ("x", "z", "yl", "yh", "core")
SEQ = ("x", "z", "yl")
DP = ("yh", "core")
NT = (((1,), (1,)), ((), ()))
TN = (((0,), (0,)), ((), ()))
F32 = jnp.float32
BF16 = jnp.bfloat16
VMEM_LIMIT = 56 * 1024 * 1024


def dot(a, b, dims=(((1,), (0,)), ((), ()))):
    return lax.dot_general(a, b, dims, preferred_element_type=F32)


def send(array, axis, size, step):
    return lax.ppermute(array, axis, [(i, (i + step) % size) for i in range(size)])


def rows_of(block):
    return jnp.concatenate(
        [block[:, h * HEAD_DIM : (h + 1) * HEAD_DIM] for h in range(HEADS)], axis=0
    )


def tiles(count):
    return [slice(t * TILE, (t + 1) * TILE) for t in range(count // TILE)]


def fold(values, op):
    return op(values.reshape(-1, 8, values.shape[1]), axis=0)


def forward_kernel(qd, kv, mixed, stats_ref, vt, *scratch):
    vt[...] = kv[:, HEAD_DIM:].T

    def scores(p, score):
        score[...] = dot(kv[:, :HEAD_DIM], rows_of(qd[p, :, :ROWS]), NT)

    def softmax(p, score, weight):
        top = jnp.full((8, ROWS), -jnp.inf, F32)
        for part in tiles(KEYS):
            top = jnp.maximum(top, fold(score[part, :], jnp.max))
        top = jnp.max(top, axis=0, keepdims=True)
        base = top * (SCALE * LOG2E)
        total = jnp.zeros((8, ROWS), F32)
        for part in tiles(KEYS):
            e = jnp.exp2(score[part, :] * (SCALE * LOG2E) - base)
            total = total + fold(e, jnp.sum)
            weight[part, :] = e.astype(BF16)
        total = jnp.sum(total, axis=0, keepdims=True)
        acc = dot(vt[...], weight[...]) * (1.0 / total)
        mixed[p] = acc.astype(BF16)
        stats_ref[pl.ds(p, 1), :] = top * SCALE + jnp.log(total)
        d4 = rows_of(qd[p, :, ROWS:])
        stats_ref[pl.ds(8 + p, 1), :] = jnp.sum(acc * d4.T.astype(F32), axis=0, keepdims=True)

    def block(i, carry):
        for n in range(2):
            scores(2 * i + n, scratch[n])
        for n in range(2):
            softmax(2 * i + n, scratch[n], scratch[2 + n])
        return carry

    lax.fori_loop(0, GROUP // 2, block, 0)


def combine(logs, bars):
    top = jnp.max(logs, axis=0)
    weights = jnp.exp(logs - top)
    total = jnp.sum(weights, axis=0)
    weights = weights / total
    return top + jnp.log(total), jnp.sum(weights * bars, axis=0), weights


def backward_kernel(qd, stats_ref, kv, dq, dkv, kt, stat, *scratch):
    kt[...] = kv[:, :HEAD_DIM].T
    logsum, delta, unused = combine(stats_ref[:, :8, :], stats_ref[:, 8:, :])
    stat[:8, :] = logsum * LOG2E
    stat[8:, :] = delta
    dkv[...] = jnp.zeros_like(dkv)

    def rows(p):
        return rows_of(qd[p, :, :ROWS]), rows_of(qd[p, :, ROWS:])

    def products(p, score, dprob):
        q4, d4 = rows(p)
        score[...] = dot(kv[:, :HEAD_DIM], q4, NT)
        dprob[...] = dot(kv[:, HEAD_DIM:], d4, NT)

    def gradients(p, score, dprob, weight, dscore):
        base = stat[pl.ds(p, 1), :]
        delta = stat[pl.ds(8 + p, 1), :]
        for tile in tiles(KEYS):
            prob = jnp.exp2(score[tile, :] * (SCALE * LOG2E) - base)
            weight[tile, :] = prob.astype(BF16)
            dscore[tile, :] = (prob * (dprob[tile, :] - delta)).astype(BF16)
        q4, d4 = rows(p)
        dkv[:, HEAD_DIM:] += dot(weight[...], d4)
        dkv[:, :HEAD_DIM] += dot(dscore[...], q4)
        dq[p] = (dot(kt[...], dscore[...]) * SCALE).astype(BF16)

    def block(i, carry):
        for n in range(2):
            products(2 * i + n, *scratch[4 * n : 4 * n + 2])
        for n in range(2):
            gradients(2 * i + n, *scratch[4 * n : 4 * n + 4])
        return carry

    lax.fori_loop(0, GROUP // 2, block, 0)
    dkv[:, :HEAD_DIM] = dkv[:, :HEAD_DIM] * SCALE


def output_kernel(place, parts, stats_ref, upstream_ref, mixed_ref, keep_ref, give_ref):
    mine = place[1]
    unused, unused, weights = combine(
        stats_ref[:, pl.ds(mine, 1), :], stats_ref[:, pl.ds(8 + mine, 1), :]
    )
    mixed_t = jnp.sum(weights * parts[...].astype(F32), axis=0)
    heads_t = [mixed_t[:, h * POS : (h + 1) * POS] for h in range(HEADS)]
    mixed_ref[...] = jnp.concatenate([m.T for m in heads_t], axis=1).astype(BF16)
    mixed_rows = jnp.concatenate(heads_t, axis=0).astype(BF16)
    half = upstream_ref.shape[1] // 2
    first = place[0] == 0
    low, high = upstream_ref[:, :half], upstream_ref[:, half:]
    keep_ref[...] = dot(mixed_rows, jnp.where(first, low, high)).astype(BF16)
    give_ref[...] = dot(mixed_rows, jnp.where(first, high, low)).astype(BF16)


def attended_kernel(tokens_ref, mixed_ref, w_out_ref, attended_ref):
    attended_ref[...] = (
        tokens_ref[...].astype(F32) + dot(mixed_ref[...], w_out_ref[...])
    ).astype(BF16)


def input_kernel(place, dq_ref, dkv_ref, both_ref, keep_ref, give_ref):
    dq_t = jnp.sum(dq_ref[...].astype(F32), axis=0)
    dquery = jnp.concatenate(
        [dq_t[:, h * POS : (h + 1) * POS].T for h in range(HEADS)], axis=1
    ).astype(BF16)
    dkeyval = dkv_ref[...].astype(BF16)
    both_ref[:, :ROWS] = dquery
    both_ref[:, ROWS:] = dkeyval
    first = place[0] == 0
    low = jnp.concatenate([dquery[:, :256], dkeyval[:, :128]], axis=1)
    high = jnp.concatenate([dquery[:, 256:], dkeyval[:, 128:]], axis=1)
    keep_ref[...] = jnp.where(first, low, high)
    give_ref[...] = jnp.where(first, high, low)


def term_kernel(tokens_ref, other_ref, keep_ref, got_ref, term_ref):
    tokens = jnp.concatenate([tokens_ref[...], other_ref[...]], axis=0)
    grads = jnp.concatenate([keep_ref[...], got_ref[...]], axis=0)
    term_ref[...] = dot(tokens, grads, TN).astype(BF16)


def tokens_kernel(both_ref, w_query_ref, w_keyval_ref, grad_ref):
    grad_ref[...] = (
        dot(both_ref[:, :ROWS], w_query_ref[...], NT)
        + dot(both_ref[:, ROWS:], w_keyval_ref[...], NT)
    ).astype(BF16)


def plus(a, b):
    return (a.astype(F32) + b.astype(F32)).astype(BF16)


VM = pl.BlockSpec(memory_space=pltpu.VMEM)
SM = pl.BlockSpec(memory_space=pltpu.SMEM)


def call(kernel, ins, outs, in_specs, out_specs, scratch, flops):
    return pl.pallas_call(
        kernel,
        out_shape=outs,
        in_specs=in_specs,
        out_specs=out_specs,
        scratch_shapes=scratch,
        compiler_params=pltpu.CompilerParams(vmem_limit_bytes=VMEM_LIMIT),
        cost_estimate=pl.CostEstimate(flops=flops, bytes_accessed=6_000_000, transcendentals=0),
    )(*ins)


def shape(*dims, dtype=BF16):
    return jax.ShapeDtypeStruct(dims, dtype)


def swap(blocks, axes):
    return lax.all_to_all(blocks, axes, 0, 0)


def share(array, axes, count):
    return swap(jnp.broadcast_to(array[None], (count,) + array.shape), axes)


def added(blocks):
    return jnp.sum(blocks.astype(F32), axis=0)


def body(tokens, upstream, w_query, w_keyval, w_out):
    local = tokens[0]
    cotangent = upstream[0]
    core = lax.axis_index("core")
    group = lax.axis_index("x") * 2 + lax.axis_index("yl")
    place = jnp.stack([core, group]).astype(jnp.int32)
    query = jnp.dot(local, w_query, preferred_element_type=F32).astype(BF16)
    dmixed = jnp.dot(cotangent, w_out.T, preferred_element_type=F32).astype(BF16)
    qd = jnp.concatenate([query, dmixed], axis=1)
    qds = share(qd, ("x", "yl"), 8)
    qd, early = lax.optimization_barrier((qd, local))
    keyval = jnp.dot(early, w_keyval, preferred_element_type=F32).astype(BF16)
    kvs = lax.all_gather(keyval, "z", axis=0, tiled=True)
    tokens_other = send(early, "core", 2, 1)
    kvs, tokens_other = lax.optimization_barrier((kvs, tokens_other))

    mixed_parts, stats = call(
        forward_kernel,
        [qds, kvs],
        [shape(8, HEAD_DIM, ROWS), shape(16, ROWS, dtype=F32)],
        [VM] * 2,
        [VM] * 2,
        [
            pltpu.VMEM((HEAD_DIM, KEYS), BF16),
            pltpu.VMEM((KEYS, ROWS), F32),
            pltpu.VMEM((KEYS, ROWS), F32),
            pltpu.VMEM((KEYS, ROWS), BF16),
            pltpu.VMEM((KEYS, ROWS), BF16),
        ],
        10_000_000_000,
    )
    all_stats = share(stats, ("x", "yl"), 8)
    mixed_parts, all_stats = lax.optimization_barrier((mixed_parts, all_stats))
    mine = swap(mixed_parts, ("x", "yl"))
    dq_parts, dkv_parts = call(
        backward_kernel,
        [qds, all_stats, kvs],
        [shape(8, HEAD_DIM, ROWS), shape(KEYS, 2 * HEAD_DIM, dtype=F32)],
        [VM] * 3,
        [VM] * 2,
        [
            pltpu.VMEM((HEAD_DIM, KEYS), BF16),
            pltpu.VMEM((16, ROWS), F32),
        ]
        + [pltpu.VMEM((KEYS, ROWS), t) for t in (F32, F32, BF16, BF16)] * 2,
        16_000_000_000,
    )
    dq_parts, mine = lax.optimization_barrier((dq_parts, mine))
    dkv = lax.psum_scatter(dkv_parts, "z", scatter_dimension=0, tiled=True)
    mixed, keep_o, give_o = call(
        output_kernel,
        [place, mine, all_stats, cotangent],
        [shape(POS, ROWS), shape(512, 768), shape(512, 768)],
        [SM] + [VM] * 3,
        [VM] * 3,
        [],
        400_000_000,
    )
    term_o = plus(keep_o, send(give_o, "core", 2, 1))
    attended = call(
        attended_kernel,
        [local, mixed, w_out],
        shape(*local.shape),
        [VM] * 3,
        VM,
        [],
        200_000_000,
    )
    term_o, attended, dq_parts = lax.optimization_barrier((term_o, attended, dq_parts))
    dqs = swap(dq_parts, ("x", "yl"))
    term_o = added(swap(term_o.reshape(4, 128, 768), "x"))
    term_o = term_o.reshape(16, 8, 2, 384).transpose(0, 2, 1, 3).reshape(16, 16, 384)
    dkv, term_o = lax.optimization_barrier((dkv, term_o))

    both, keep_i, give_i = call(
        input_kernel,
        [place, dqs, dkv],
        [shape(POS, 768), shape(POS, 384), shape(POS, 384)],
        [SM] + [VM] * 2,
        [VM] * 3,
        [],
        10_000_000,
    )
    term_i = call(
        term_kernel,
        [local, tokens_other, keep_i, send(give_i, "core", 2, 1)],
        shape(1536, 384),
        [VM] * 4,
        VM,
        [],
        300_000_000,
    )
    grad_tokens = call(
        tokens_kernel,
        [both, w_query, w_keyval],
        shape(*local.shape),
        [VM] * 3,
        VM,
        [],
        300_000_000,
    )
    term_i = swap(term_i.reshape(4, 384, 384), "x")
    grad_tokens, term_i = lax.optimization_barrier((grad_tokens, term_i))
    term_i = added(term_i)
    ends = jnp.concatenate([term_i.reshape(16, 24, 384), term_o], axis=1).astype(BF16)
    ends = swap(ends, ("z", "yl"))
    ends = added(ends)
    ends = ends + send(ends, "yh", 2, 1)
    other = send(ends, "core", 2, 1)
    low, high = jnp.where(core == 0, ends, other), jnp.where(core == 0, other, ends)
    grad_o = jnp.stack([low[24:], high[24:]]).reshape(2, 2, 8, 384)
    grad_o = grad_o.transpose(2, 0, 1, 3).reshape(8, 1536)
    return (
        attended[None],
        grad_tokens[None],
        jnp.concatenate([low[:24, :256], high[:24, :256]], axis=1),
        jnp.concatenate([low[:24, 256:], high[:24, 256:]], axis=1),
        grad_o,
    )


def solution(mesh):
    torus = Mesh(mesh.devices.reshape(4, 8, 2, 2, 2), AXES)
    return jax.shard_map(
        body,
        mesh=torus,
        in_specs=(P(DP, SEQ, None), P(DP, SEQ, None), P(), P(), P()),
        out_specs=(
            P(DP, SEQ, None),
            P(DP, SEQ, None),
            P(SEQ, None),
            P(SEQ, None),
            P(SEQ, None),
        ),
        check_vma=False,
    )
```

```python
import math

import jax
import jax.numpy as jnp
from jax import lax
from jax.experimental import pallas as pl
from jax.experimental.pallas import tpu as pltpu
from jax.sharding import Mesh, PartitionSpec as P

HEADS = 4
HEAD_DIM = 128
POS = 128
ROWS = HEADS * POS
GROUP = 8
KEYS = 8 * POS
TILE = 32
SCALE = 1.0 / HEAD_DIM**0.5
LOG2E = math.log2(math.e)
AXES = ("x", "z", "yl", "yh", "core")
SEQ = ("x", "z", "yl")
DP = ("yh", "core")
NT = (((1,), (1,)), ((), ()))
TN = (((0,), (0,)), ((), ()))
F32 = jnp.float32
BF16 = jnp.bfloat16
VMEM_LIMIT = 56 * 1024 * 1024


def dot(a, b, dims=(((1,), (0,)), ((), ()))):
    return lax.dot_general(a, b, dims, preferred_element_type=F32)


def send(array, axis, size, step):
    return lax.ppermute(array, axis, [(i, (i + step) % size) for i in range(size)])


def send_y(array, step_l, step_h):
    pairs = [
        (a * 2 + b, (a + step_l) % 2 * 2 + (b + step_h) % 2) for a in range(2) for b in range(2)
    ]
    return lax.ppermute(array, ("yl", "yh"), pairs)


def rows_of(block):
    return jnp.concatenate(
        [block[:, h * HEAD_DIM : (h + 1) * HEAD_DIM] for h in range(HEADS)], axis=0
    )


def tiles(count):
    return [slice(t * TILE, (t + 1) * TILE) for t in range(count // TILE)]


def fold(values, op):
    return op(values.reshape(-1, 8, values.shape[1]), axis=0)


def forward_kernel(qd, kv, mixed, stats_out, vt, stats_ref, *scratch):
    vt[...] = kv[:, HEAD_DIM:].T

    def scores(p, score):
        score[...] = dot(kv[:, :HEAD_DIM], rows_of(qd[p, :, :ROWS]), NT)

    def softmax(p, score, weight):
        top = jnp.full((8, ROWS), -jnp.inf, F32)
        for part in tiles(KEYS):
            top = jnp.maximum(top, fold(score[part, :], jnp.max))
        top = jnp.max(top, axis=0, keepdims=True)
        base = top * (SCALE * LOG2E)
        total = jnp.zeros((8, ROWS), F32)
        for part in tiles(KEYS):
            e = jnp.exp2(score[part, :] * (SCALE * LOG2E) - base)
            total = total + fold(e, jnp.sum)
            weight[part, :] = e.astype(BF16)
        total = jnp.sum(total, axis=0, keepdims=True)
        acc = dot(vt[...], weight[...]) * (1.0 / total)
        mixed[p] = acc.astype(BF16)
        stats_ref[pl.ds(p, 1), :] = top * SCALE + jnp.log(total)
        d4 = rows_of(qd[p, :, ROWS:])
        stats_ref[pl.ds(8 + p, 1), :] = jnp.sum(acc * d4.T.astype(F32), axis=0, keepdims=True)

    def block(i, carry):
        for n in range(2):
            scores(2 * i + n, scratch[n])
        for n in range(2):
            softmax(2 * i + n, scratch[n], scratch[2 + n])
        return carry

    lax.fori_loop(0, GROUP // 2, block, 0)
    for i in range(GROUP):
        stats_out[i] = stats_ref[...]


def combine(logs, bars):
    top = jnp.max(logs, axis=0)
    weights = jnp.exp(logs - top)
    total = jnp.sum(weights, axis=0)
    weights = weights / total
    return top + jnp.log(total), jnp.sum(weights * bars, axis=0), weights


def backward_kernel(qd, stats_ref, kv, dq, dkv, kt, stat, *scratch):
    kt[...] = kv[:, :HEAD_DIM].T
    logsum, delta, unused = combine(stats_ref[:, :8, :], stats_ref[:, 8:, :])
    stat[:8, :] = logsum * LOG2E
    stat[8:, :] = delta
    dkv[...] = jnp.zeros_like(dkv)

    def rows(p):
        return rows_of(qd[p, :, :ROWS]), rows_of(qd[p, :, ROWS:])

    def products(p, score, dprob):
        q4, d4 = rows(p)
        score[...] = dot(kv[:, :HEAD_DIM], q4, NT)
        dprob[...] = dot(kv[:, HEAD_DIM:], d4, NT)

    def gradients(p, score, dprob, weight, dscore):
        base = stat[pl.ds(p, 1), :]
        delta = stat[pl.ds(8 + p, 1), :]
        for tile in tiles(KEYS):
            prob = jnp.exp2(score[tile, :] * (SCALE * LOG2E) - base)
            weight[tile, :] = prob.astype(BF16)
            dscore[tile, :] = (prob * (dprob[tile, :] - delta)).astype(BF16)
        q4, d4 = rows(p)
        dkv[:, HEAD_DIM:] += dot(weight[...], d4)
        dkv[:, :HEAD_DIM] += dot(dscore[...], q4)
        dq[p] = (dot(kt[...], dscore[...]) * SCALE).astype(BF16)

    def block(i, carry):
        for n in range(2):
            products(2 * i + n, *scratch[4 * n : 4 * n + 2])
        for n in range(2):
            gradients(2 * i + n, *scratch[4 * n : 4 * n + 4])
        return carry

    lax.fori_loop(0, GROUP // 2, block, 0)
    dkv[:, :HEAD_DIM] = dkv[:, :HEAD_DIM] * SCALE


def output_kernel(place, parts, stats_ref, upstream_ref, mixed_ref, keep_ref, give_ref):
    mine = place[1]
    unused, unused, weights = combine(
        stats_ref[:, pl.ds(mine, 1), :], stats_ref[:, pl.ds(8 + mine, 1), :]
    )
    mixed_t = jnp.sum(weights * parts[...].astype(F32), axis=0)
    heads_t = [mixed_t[:, h * POS : (h + 1) * POS] for h in range(HEADS)]
    mixed_ref[...] = jnp.concatenate([m.T for m in heads_t], axis=1).astype(BF16)
    mixed_rows = jnp.concatenate(heads_t, axis=0).astype(BF16)
    half = upstream_ref.shape[1] // 2
    first = place[0] == 0
    low, high = upstream_ref[:, :half], upstream_ref[:, half:]
    keep_ref[...] = dot(mixed_rows, jnp.where(first, low, high)).astype(BF16)
    give_ref[...] = dot(mixed_rows, jnp.where(first, high, low)).astype(BF16)


def attended_kernel(tokens_ref, mixed_ref, w_out_ref, attended_ref):
    attended_ref[...] = (
        tokens_ref[...].astype(F32) + dot(mixed_ref[...], w_out_ref[...])
    ).astype(BF16)


def input_kernel(place, dq_ref, dkv_ref, both_ref, keep_ref, give_ref):
    dq_t = jnp.sum(dq_ref[...].astype(F32), axis=0)
    dquery = jnp.concatenate(
        [dq_t[:, h * POS : (h + 1) * POS].T for h in range(HEADS)], axis=1
    ).astype(BF16)
    dkeyval = dkv_ref[...].astype(BF16)
    both_ref[:, :ROWS] = dquery
    both_ref[:, ROWS:] = dkeyval
    first = place[0] == 0
    low = jnp.concatenate([dquery[:, :256], dkeyval[:, :128]], axis=1)
    high = jnp.concatenate([dquery[:, 256:], dkeyval[:, 128:]], axis=1)
    keep_ref[...] = jnp.where(first, low, high)
    give_ref[...] = jnp.where(first, high, low)


def term_kernel(tokens_ref, other_ref, keep_ref, got_ref, term_ref):
    tokens = jnp.concatenate([tokens_ref[...], other_ref[...]], axis=0)
    grads = jnp.concatenate([keep_ref[...], got_ref[...]], axis=0)
    term_ref[...] = dot(tokens, grads, TN).astype(BF16)


def tokens_kernel(both_ref, w_query_ref, w_keyval_ref, grad_ref):
    grad_ref[...] = (
        dot(both_ref[:, :ROWS], w_query_ref[...], NT)
        + dot(both_ref[:, ROWS:], w_keyval_ref[...], NT)
    ).astype(BF16)


def plus(a, b):
    return (a.astype(F32) + b.astype(F32)).astype(BF16)


VM = pl.BlockSpec(memory_space=pltpu.VMEM)
SM = pl.BlockSpec(memory_space=pltpu.SMEM)


def call(kernel, ins, outs, in_specs, out_specs, scratch, flops):
    return pl.pallas_call(
        kernel,
        out_shape=outs,
        in_specs=in_specs,
        out_specs=out_specs,
        scratch_shapes=scratch,
        compiler_params=pltpu.CompilerParams(vmem_limit_bytes=VMEM_LIMIT),
        cost_estimate=pl.CostEstimate(flops=flops, bytes_accessed=6_000_000, transcendentals=0),
    )(*ins)


def shape(*dims, dtype=BF16):
    return jax.ShapeDtypeStruct(dims, dtype)


def swap(blocks, axes):
    return lax.all_to_all(blocks, axes, 0, 0)


def share(array, axes, count):
    return swap(jnp.broadcast_to(array[None], (count,) + array.shape), axes)


def added(blocks):
    return jnp.sum(blocks.astype(F32), axis=0)


def body(tokens, upstream, w_query, w_keyval, w_out):
    local = tokens[0]
    cotangent = upstream[0]
    core = lax.axis_index("core")
    group = lax.axis_index("x") * 2 + lax.axis_index("yl")
    place = jnp.stack([core, group]).astype(jnp.int32)
    query = jnp.dot(local, w_query, preferred_element_type=F32).astype(BF16)
    dmixed = jnp.dot(cotangent, w_out.T, preferred_element_type=F32).astype(BF16)
    qd = jnp.concatenate([query, dmixed], axis=1)
    qds = share(qd, ("x", "yl"), 8)
    qd, early = lax.optimization_barrier((qd, local))
    keyval = jnp.dot(early, w_keyval, preferred_element_type=F32).astype(BF16)
    kvs = lax.all_gather(keyval, "z", axis=0, tiled=True)
    tokens_other = send(early, "core", 2, 1)
    kvs, tokens_other, place = lax.optimization_barrier((kvs, tokens_other, place))

    mixed_parts, stats = call(
        forward_kernel,
        [qds, kvs],
        [shape(8, HEAD_DIM, ROWS), shape(8, 16, ROWS, dtype=F32)],
        [VM] * 2,
        [VM] * 2,
        [
            pltpu.VMEM((HEAD_DIM, KEYS), BF16),
            pltpu.VMEM((16, ROWS), F32),
            pltpu.VMEM((KEYS, ROWS), F32),
            pltpu.VMEM((KEYS, ROWS), F32),
            pltpu.VMEM((KEYS, ROWS), BF16),
            pltpu.VMEM((KEYS, ROWS), BF16),
        ],
        10_000_000_000,
    )
    all_stats = swap(stats, ("x", "yl"))
    mixed_parts, all_stats = lax.optimization_barrier((mixed_parts, all_stats))
    mine = swap(mixed_parts, ("x", "yl"))
    dq_parts, dkv_parts = call(
        backward_kernel,
        [qds, all_stats, kvs],
        [shape(8, HEAD_DIM, ROWS), shape(KEYS, 2 * HEAD_DIM, dtype=F32)],
        [VM] * 3,
        [VM] * 2,
        [
            pltpu.VMEM((HEAD_DIM, KEYS), BF16),
            pltpu.VMEM((16, ROWS), F32),
        ]
        + [pltpu.VMEM((KEYS, ROWS), t) for t in (F32, F32, BF16, BF16)] * 2,
        16_000_000_000,
    )
    dq_parts, mine = lax.optimization_barrier((dq_parts, mine))
    dkv = lax.psum_scatter(dkv_parts, "z", scatter_dimension=0, tiled=True)
    mixed, keep_o, give_o = call(
        output_kernel,
        [place, mine, all_stats, cotangent],
        [shape(POS, ROWS), shape(512, 768), shape(512, 768)],
        [SM] + [VM] * 3,
        [VM] * 3,
        [],
        400_000_000,
    )
    term_o = plus(keep_o, send(give_o, "core", 2, 1))
    attended = call(
        attended_kernel,
        [local, mixed, w_out],
        shape(*local.shape),
        [VM] * 3,
        VM,
        [],
        20_000_000_000,
    )
    term_o, attended, dq_parts = lax.optimization_barrier((term_o, attended, dq_parts))
    dqs = swap(dq_parts, ("x", "yl"))
    term_o = swap(term_o.reshape(4, 128, 768), "x")
    dqs, term_o = lax.optimization_barrier((dqs, term_o))

    both, keep_i, give_i = call(
        input_kernel,
        [place, dqs, dkv],
        [shape(POS, 768), shape(POS, 384), shape(POS, 384)],
        [SM] + [VM] * 2,
        [VM] * 3,
        [],
        10_000_000,
    )
    term_i = call(
        term_kernel,
        [local, tokens_other, keep_i, send(give_i, "core", 2, 1)],
        shape(1536, 384),
        [VM] * 4,
        VM,
        [],
        300_000_000,
    )
    grad_tokens = call(
        tokens_kernel,
        [both, w_query, w_keyval],
        shape(*local.shape),
        [VM] * 3,
        VM,
        [],
        300_000_000,
    )
    yl, yh = lax.axis_index("yl"), lax.axis_index("yh")
    blocks = added(term_o).astype(BF16).reshape(8, 2, 8, 2, 384)
    blocks = blocks.transpose(1, 3, 0, 2, 4).reshape(4, 64, 384)

    def block(step_l, step_h):
        at = (yl + step_l) % 2 * 2 + (yh + step_h) % 2
        return lax.dynamic_index_in_dim(blocks, at, 0, keepdims=False)

    steps = [(0, 1), (1, 0), (1, 1)]
    term_o = block(0, 0).astype(F32)
    term_o = term_o + sum(send_y(block(*step), *step).astype(F32) for step in steps)
    term_i = swap(term_i.reshape(4, 384, 384), "x")
    grad_tokens, term_i, term_o = lax.optimization_barrier((grad_tokens, term_i, term_o))
    term_i = added(term_i).reshape(8, 2, 24, 384)
    here = (jnp.arange(2) == lax.axis_index("yl"))[None, :, None, None]
    term_o = jnp.where(here, term_o.reshape(8, 1, 8, 384), 0.0)
    ends = jnp.concatenate([term_i, term_o], axis=2).astype(BF16).reshape(16, 32, 384)
    ends = added(swap(ends, ("z", "yl")))
    got = send(ends, "yh", 2, 1)
    ends = jnp.concatenate(
        [
            ends[:24] + got[:24],
            jnp.where(yh == 0, ends[24:], got[24:]),
            jnp.where(yh == 0, got[24:], ends[24:]),
        ]
    )
    other = send(ends, "core", 2, 1)
    low, high = jnp.where(core == 0, ends, other), jnp.where(core == 0, other, ends)
    grad_o = jnp.concatenate([low[24:32], low[32:], high[24:32], high[32:]], axis=1)
    return (
        attended[None],
        grad_tokens[None],
        jnp.concatenate([low[:24, :256], high[:24, :256]], axis=1),
        jnp.concatenate([low[:24, 256:], high[:24, 256:]], axis=1),
        grad_o,
    )


def solution(mesh):
    torus = Mesh(mesh.devices.reshape(4, 8, 2, 2, 2), AXES)
    return jax.shard_map(
        body,
        mesh=torus,
        in_specs=(P(DP, SEQ, None), P(DP, SEQ, None), P(), P(), P()),
        out_specs=(
            P(DP, SEQ, None),
            P(DP, SEQ, None),
            P(SEQ, None),
            P(SEQ, None),
            P(SEQ, None),
        ),
        check_vma=False,
    )
```

```python
import math

import jax
import jax.numpy as jnp
from jax import lax
from jax.experimental import pallas as pl
from jax.experimental.pallas import tpu as pltpu
from jax.sharding import Mesh, PartitionSpec as P

HEADS = 4
HEAD_DIM = 128
POS = 128
ROWS = HEADS * POS
GROUP = 8
KEYS = 8 * POS
TILE = 32
SCALE = 1.0 / HEAD_DIM**0.5
LOG2E = math.log2(math.e)
AXES = ("x", "z", "yl", "yh", "core")
SEQ = ("x", "z", "yl")
DP = ("yh", "core")
NT = (((1,), (1,)), ((), ()))
TN = (((0,), (0,)), ((), ()))
F32 = jnp.float32
BF16 = jnp.bfloat16
VMEM_LIMIT = 56 * 1024 * 1024


def dot(a, b, dims=(((1,), (0,)), ((), ()))):
    return lax.dot_general(a, b, dims, preferred_element_type=F32)


def send(array, axis, size, step):
    return lax.ppermute(array, axis, [(i, (i + step) % size) for i in range(size)])


def send_y(array, step_l, step_h):
    pairs = [
        (a * 2 + b, (a + step_l) % 2 * 2 + (b + step_h) % 2) for a in range(2) for b in range(2)
    ]
    return lax.ppermute(array, ("yl", "yh"), pairs)


def rows_of(block):
    return jnp.concatenate(
        [block[:, h * HEAD_DIM : (h + 1) * HEAD_DIM] for h in range(HEADS)], axis=0
    )


def tiles(count):
    return [slice(t * TILE, (t + 1) * TILE) for t in range(count // TILE)]


def fold(values, op):
    return op(values.reshape(-1, 8, values.shape[1]), axis=0)


def forward_kernel(qd, kv, mixed, stats_out, tops, kept, vt, stats_ref, sem, *scratch):
    vt[...] = kv[:, HEAD_DIM:].T

    def scores(p, score):
        score[...] = dot(kv[:, :HEAD_DIM], rows_of(qd[p, :, :ROWS]), NT)

    def softmax(p, score, weight):
        top = jnp.full((8, ROWS), -jnp.inf, F32)
        for part in tiles(KEYS):
            top = jnp.maximum(top, fold(score[part, :], jnp.max))
        top = jnp.max(top, axis=0, keepdims=True)
        base = top * (SCALE * LOG2E)
        tops[pl.ds(p, 1), :] = top * SCALE
        total = jnp.zeros((8, ROWS), F32)
        for part in tiles(KEYS):
            e = jnp.exp2(score[part, :] * (SCALE * LOG2E) - base)
            total = total + fold(e, jnp.sum)
            weight[part, :] = e.astype(BF16)
        total = jnp.sum(total, axis=0, keepdims=True)
        acc = dot(vt[...], weight[...]) * (1.0 / total)
        mixed[p] = acc.astype(BF16)
        stats_ref[pl.ds(p, 1), :] = top * SCALE + jnp.log(total)
        d4 = rows_of(qd[p, :, ROWS:])
        stats_ref[pl.ds(8 + p, 1), :] = jnp.sum(acc * d4.T.astype(F32), axis=0, keepdims=True)

    def keep(p, n):
        return pltpu.make_async_copy(scratch[2 + n], kept.at[p], sem.at[n])

    def block(i, carry):
        for n in range(2):
            scores(2 * i + n, scratch[n])
        for n in range(2):

            @pl.when(i > 0)
            def _():
                keep(2 * i + n - 2, n).wait()

            softmax(2 * i + n, scratch[n], scratch[2 + n])
            keep(2 * i + n, n).start()
        return carry

    lax.fori_loop(0, GROUP // 2, block, 0)
    for n in range(2):
        keep(GROUP - 2 + n, n).wait()
    for i in range(GROUP):
        stats_out[i] = stats_ref[...]


def combine(logs, bars):
    top = jnp.max(logs, axis=0)
    weights = jnp.exp(logs - top)
    total = jnp.sum(weights, axis=0)
    weights = weights / total
    return top + jnp.log(total), jnp.sum(weights * bars, axis=0), weights


def backward_kernel(qd, stats_ref, tops, kv, kept, dq, dkv, kt, stat, held, sem, *scratch):
    def fetch(p, slot):
        return pltpu.make_async_copy(kept.at[p], held.at[slot], sem.at[slot])

    for n in range(2):
        fetch(n, n).start()
    kt[...] = kv[:, :HEAD_DIM].T
    logsum, delta, unused = combine(stats_ref[:, :8, :], stats_ref[:, 8:, :])
    stat[:8, :] = jnp.exp(tops[...] - logsum)
    stat[8:, :] = delta
    dkv[...] = jnp.zeros_like(dkv)

    def rows(p, first):
        return rows_of(qd[p, :, first : first + ROWS])

    def gradients(p, slot, dprob, weight, dscore):
        share_here = stat[pl.ds(p, 1), :]
        delta = stat[pl.ds(8 + p, 1), :]
        for tile in tiles(KEYS):
            prob = held[slot, tile, :].astype(F32) * share_here
            weight[tile, :] = prob.astype(BF16)
            dscore[tile, :] = (prob * (dprob[tile, :] - delta)).astype(BF16)
        dkv[:, HEAD_DIM:] += dot(weight[...], rows(p, ROWS))
        dkv[:, :HEAD_DIM] += dot(dscore[...], rows(p, 0))
        dq[p] = (dot(kt[...], dscore[...]) * SCALE).astype(BF16)

    def block(i, carry):
        slot = i % 2 * 2

        @pl.when(i + 1 < GROUP // 2)
        def _():
            for n in range(2):
                fetch(2 * i + 2 + n, 2 - slot + n).start()

        for n in range(2):
            scratch[3 * n][...] = dot(kv[:, HEAD_DIM:], rows(2 * i + n, ROWS), NT)
        for n in range(2):
            fetch(2 * i + n, slot + n).wait()
        for n in range(2):
            gradients(2 * i + n, slot + n, *scratch[3 * n : 3 * n + 3])
        return carry

    lax.fori_loop(0, GROUP // 2, block, 0)
    dkv[:, :HEAD_DIM] = dkv[:, :HEAD_DIM] * SCALE


def output_kernel(place, parts, stats_ref, upstream_ref, mixed_ref, keep_ref, give_ref):
    mine = place[1]
    unused, unused, weights = combine(
        stats_ref[:, pl.ds(mine, 1), :], stats_ref[:, pl.ds(8 + mine, 1), :]
    )
    mixed_t = jnp.sum(weights * parts[...].astype(F32), axis=0)
    heads_t = [mixed_t[:, h * POS : (h + 1) * POS] for h in range(HEADS)]
    mixed_ref[...] = jnp.concatenate([m.T for m in heads_t], axis=1).astype(BF16)
    mixed_rows = jnp.concatenate(heads_t, axis=0).astype(BF16)
    half = upstream_ref.shape[1] // 2
    first = place[0] == 0
    low, high = upstream_ref[:, :half], upstream_ref[:, half:]
    keep_ref[...] = dot(mixed_rows, jnp.where(first, low, high)).astype(BF16)
    give_ref[...] = dot(mixed_rows, jnp.where(first, high, low)).astype(BF16)


def attended_kernel(tokens_ref, mixed_ref, w_out_ref, attended_ref):
    attended_ref[...] = (
        tokens_ref[...].astype(F32) + dot(mixed_ref[...], w_out_ref[...])
    ).astype(BF16)


def input_kernel(place, dq_ref, dkv_ref, both_ref, keep_ref, give_ref):
    dq_t = jnp.sum(dq_ref[...].astype(F32), axis=0)
    dquery = jnp.concatenate(
        [dq_t[:, h * POS : (h + 1) * POS].T for h in range(HEADS)], axis=1
    ).astype(BF16)
    dkeyval = dkv_ref[...].astype(BF16)
    both_ref[:, :ROWS] = dquery
    both_ref[:, ROWS:] = dkeyval
    first = place[0] == 0
    low = jnp.concatenate([dquery[:, :256], dkeyval[:, :128]], axis=1)
    high = jnp.concatenate([dquery[:, 256:], dkeyval[:, 128:]], axis=1)
    keep_ref[...] = jnp.where(first, low, high)
    give_ref[...] = jnp.where(first, high, low)


def term_kernel(tokens_ref, other_ref, keep_ref, got_ref, term_ref):
    tokens = jnp.concatenate([tokens_ref[...], other_ref[...]], axis=0)
    grads = jnp.concatenate([keep_ref[...], got_ref[...]], axis=0)
    term_ref[...] = dot(tokens, grads, TN).astype(BF16)


def tokens_kernel(both_ref, w_query_ref, w_keyval_ref, grad_ref):
    grad_ref[...] = (
        dot(both_ref[:, :ROWS], w_query_ref[...], NT)
        + dot(both_ref[:, ROWS:], w_keyval_ref[...], NT)
    ).astype(BF16)


def plus(a, b):
    return (a.astype(F32) + b.astype(F32)).astype(BF16)


VM = pl.BlockSpec(memory_space=pltpu.VMEM)
SM = pl.BlockSpec(memory_space=pltpu.SMEM)
HB = pl.BlockSpec(memory_space=pl.ANY)


def call(kernel, ins, outs, in_specs, out_specs, scratch, flops):
    return pl.pallas_call(
        kernel,
        out_shape=outs,
        in_specs=in_specs,
        out_specs=out_specs,
        scratch_shapes=scratch,
        compiler_params=pltpu.CompilerParams(vmem_limit_bytes=VMEM_LIMIT),
        cost_estimate=pl.CostEstimate(flops=flops, bytes_accessed=6_000_000, transcendentals=0),
    )(*ins)


def shape(*dims, dtype=BF16):
    return jax.ShapeDtypeStruct(dims, dtype)


def swap(blocks, axes):
    return lax.all_to_all(blocks, axes, 0, 0)


def share(array, axes, count):
    return swap(jnp.broadcast_to(array[None], (count,) + array.shape), axes)


def added(blocks):
    return jnp.sum(blocks.astype(F32), axis=0)


def body(tokens, upstream, w_query, w_keyval, w_out):
    local = tokens[0]
    cotangent = upstream[0]
    core = lax.axis_index("core")
    group = lax.axis_index("x") * 2 + lax.axis_index("yl")
    place = jnp.stack([core, group]).astype(jnp.int32)
    query = jnp.dot(local, w_query, preferred_element_type=F32).astype(BF16)
    dmixed = jnp.dot(cotangent, w_out.T, preferred_element_type=F32).astype(BF16)
    qd = jnp.concatenate([query, dmixed], axis=1)
    qds = share(qd, ("x", "yl"), 8)
    qd, early = lax.optimization_barrier((qd, local))
    keyval = jnp.dot(early, w_keyval, preferred_element_type=F32).astype(BF16)
    kvs = lax.all_gather(keyval, "z", axis=0, tiled=True)
    tokens_other = send(early, "core", 2, 1)
    kvs, tokens_other, place = lax.optimization_barrier((kvs, tokens_other, place))

    mixed_parts, stats, tops, kept = call(
        forward_kernel,
        [qds, kvs],
        [
            shape(8, HEAD_DIM, ROWS),
            shape(8, 16, ROWS, dtype=F32),
            shape(8, ROWS, dtype=F32),
            shape(8, KEYS, ROWS),
        ],
        [VM] * 2,
        [VM] * 3 + [HB],
        [
            pltpu.VMEM((HEAD_DIM, KEYS), BF16),
            pltpu.VMEM((16, ROWS), F32),
            pltpu.SemaphoreType.DMA((2,)),
            pltpu.VMEM((KEYS, ROWS), F32),
            pltpu.VMEM((KEYS, ROWS), F32),
            pltpu.VMEM((KEYS, ROWS), BF16),
            pltpu.VMEM((KEYS, ROWS), BF16),
        ],
        10_000_000_000,
    )
    all_stats = swap(stats, ("x", "yl"))
    mixed_parts, all_stats = lax.optimization_barrier((mixed_parts, all_stats))
    mine = swap(mixed_parts, ("x", "yl"))
    dq_parts, dkv_parts = call(
        backward_kernel,
        [qds, all_stats, tops, kvs, kept],
        [shape(8, HEAD_DIM, ROWS), shape(KEYS, 2 * HEAD_DIM, dtype=F32)],
        [VM] * 4 + [HB],
        [VM] * 2,
        [
            pltpu.VMEM((HEAD_DIM, KEYS), BF16),
            pltpu.VMEM((16, ROWS), F32),
            pltpu.VMEM((4, KEYS, ROWS), BF16),
            pltpu.SemaphoreType.DMA((4,)),
        ]
        + [pltpu.VMEM((KEYS, ROWS), t) for t in (F32, BF16, BF16)] * 2,
        16_000_000_000,
    )
    dq_parts, mine = lax.optimization_barrier((dq_parts, mine))
    dkv = lax.psum_scatter(dkv_parts, "z", scatter_dimension=0, tiled=True)
    mixed, keep_o, give_o = call(
        output_kernel,
        [place, mine, all_stats, cotangent],
        [shape(POS, ROWS), shape(512, 768), shape(512, 768)],
        [SM] + [VM] * 3,
        [VM] * 3,
        [],
        400_000_000,
    )
    term_o = plus(keep_o, send(give_o, "core", 2, 1))
    attended = call(
        attended_kernel,
        [local, mixed, w_out],
        shape(*local.shape),
        [VM] * 3,
        VM,
        [],
        20_000_000_000,
    )
    term_o, attended, dq_parts = lax.optimization_barrier((term_o, attended, dq_parts))
    dqs = swap(dq_parts, ("x", "yl"))
    term_o = swap(term_o.reshape(4, 128, 768), "x")
    dqs, term_o = lax.optimization_barrier((dqs, term_o))

    both, keep_i, give_i = call(
        input_kernel,
        [place, dqs, dkv],
        [shape(POS, 768), shape(POS, 384), shape(POS, 384)],
        [SM] + [VM] * 2,
        [VM] * 3,
        [],
        10_000_000,
    )
    term_i = call(
        term_kernel,
        [local, tokens_other, keep_i, send(give_i, "core", 2, 1)],
        shape(1536, 384),
        [VM] * 4,
        VM,
        [],
        300_000_000,
    )
    grad_tokens = call(
        tokens_kernel,
        [both, w_query, w_keyval],
        shape(*local.shape),
        [VM] * 3,
        VM,
        [],
        300_000_000,
    )
    yl, yh = lax.axis_index("yl"), lax.axis_index("yh")
    blocks = added(term_o).astype(BF16).reshape(8, 2, 8, 2, 384)
    blocks = blocks.transpose(1, 3, 0, 2, 4).reshape(4, 64, 384)

    def block(step_l, step_h):
        at = (yl + step_l) % 2 * 2 + (yh + step_h) % 2
        return lax.dynamic_index_in_dim(blocks, at, 0, keepdims=False)

    steps = [(0, 1), (1, 0), (1, 1)]
    term_o = block(0, 0).astype(F32)
    term_o = term_o + sum(send_y(block(*step), *step).astype(F32) for step in steps)
    term_i = swap(term_i.reshape(4, 384, 384), "x")
    grad_tokens, term_i, term_o = lax.optimization_barrier((grad_tokens, term_i, term_o))
    term_i = added(term_i).reshape(8, 2, 24, 384)
    here = (jnp.arange(2) == lax.axis_index("yl"))[None, :, None, None]
    term_o = jnp.where(here, term_o.reshape(8, 1, 8, 384), 0.0)
    ends = jnp.concatenate([term_i, term_o], axis=2).astype(BF16).reshape(16, 32, 384)
    ends = added(swap(ends, ("z", "yl")))
    got = send(ends, "yh", 2, 1)
    ends = jnp.concatenate(
        [
            ends[:24] + got[:24],
            jnp.where(yh == 0, ends[24:], got[24:]),
            jnp.where(yh == 0, got[24:], ends[24:]),
        ]
    )
    other = send(ends, "core", 2, 1)
    low, high = jnp.where(core == 0, ends, other), jnp.where(core == 0, other, ends)
    grad_o = jnp.concatenate([low[24:32], low[32:], high[24:32], high[32:]], axis=1)
    return (
        attended[None],
        grad_tokens[None],
        jnp.concatenate([low[:24, :256], high[:24, :256]], axis=1),
        jnp.concatenate([low[:24, 256:], high[:24, 256:]], axis=1),
        grad_o,
    )


def solution(mesh):
    torus = Mesh(mesh.devices.reshape(4, 8, 2, 2, 2), AXES)
    return jax.shard_map(
        body,
        mesh=torus,
        in_specs=(P(DP, SEQ, None), P(DP, SEQ, None), P(), P(), P()),
        out_specs=(
            P(DP, SEQ, None),
            P(DP, SEQ, None),
            P(SEQ, None),
            P(SEQ, None),
            P(SEQ, None),
        ),
        check_vma=False,
    )
```

```python
import math

import jax
import jax.numpy as jnp
from jax import lax
from jax.experimental import pallas as pl
from jax.experimental.pallas import tpu as pltpu
from jax.sharding import Mesh, PartitionSpec as P

HEADS = 4
HEAD_DIM = 128
POS = 128
ROWS = HEADS * POS
GROUP = 8
KEYS = 8 * POS
TILE = 16
SCALE = 1.0 / HEAD_DIM**0.5
LOG2E = math.log2(math.e)
AXES = ("x", "z", "yl", "yh", "core")
SEQ = ("x", "z", "yl")
DP = ("yh", "core")
NT = (((1,), (1,)), ((), ()))
TN = (((0,), (0,)), ((), ()))
F32 = jnp.float32
BF16 = jnp.bfloat16
VMEM_LIMIT = 56 * 1024 * 1024


def dot(a, b, dims=(((1,), (0,)), ((), ()))):
    return lax.dot_general(a, b, dims, preferred_element_type=F32)


def send(array, axis, size, step):
    return lax.ppermute(array, axis, [(i, (i + step) % size) for i in range(size)])


def send_y(array, step_l, step_h):
    pairs = [
        (a * 2 + b, (a + step_l) % 2 * 2 + (b + step_h) % 2) for a in range(2) for b in range(2)
    ]
    return lax.ppermute(array, ("yl", "yh"), pairs)


def rows_of(block):
    return jnp.concatenate(
        [block[:, h * HEAD_DIM : (h + 1) * HEAD_DIM] for h in range(HEADS)], axis=0
    )


def tiles(count):
    return [slice(t * TILE, (t + 1) * TILE) for t in range(count // TILE)]


def fold(values, op):
    return op(values.reshape(-1, 8, values.shape[1]), axis=0)


def forward_kernel(qd, kv, mixed, stats_out, vt, stats_ref, *scratch):
    vt[...] = kv[:, HEAD_DIM:].T

    def scores(p, score):
        score[...] = dot(kv[:, :HEAD_DIM], rows_of(qd[p, :, :ROWS]), NT)

    def softmax(p, score, weight):
        top = jnp.full((8, ROWS), -jnp.inf, F32)
        for part in tiles(KEYS):
            top = jnp.maximum(top, fold(score[part, :], jnp.max))
        top = jnp.max(top, axis=0, keepdims=True)
        base = top * (SCALE * LOG2E)
        total = jnp.zeros((8, ROWS), F32)
        for part in tiles(KEYS):
            e = jnp.exp2(score[part, :] * (SCALE * LOG2E) - base)
            total = total + fold(e, jnp.sum)
            weight[part, :] = e.astype(BF16)
        total = jnp.sum(total, axis=0, keepdims=True)
        acc = dot(vt[...], weight[...]) * (1.0 / total)
        mixed[p] = acc.astype(BF16)
        stats_ref[pl.ds(p, 1), :] = top * SCALE + jnp.log(total)
        d4 = rows_of(qd[p, :, ROWS:])
        stats_ref[pl.ds(8 + p, 1), :] = jnp.sum(acc * d4.T.astype(F32), axis=0, keepdims=True)

    def block(i, carry):
        for n in range(2):
            scores(2 * i + n, scratch[n])
        for n in range(2):
            softmax(2 * i + n, scratch[n], scratch[2 + n])
        return carry

    lax.fori_loop(0, GROUP // 2, block, 0)
    for i in range(GROUP):
        stats_out[i] = stats_ref[...]


def combine(logs, bars):
    top = jnp.max(logs, axis=0)
    weights = jnp.exp(logs - top)
    total = jnp.sum(weights, axis=0)
    weights = weights / total
    return top + jnp.log(total), jnp.sum(weights * bars, axis=0), weights


def backward_kernel(qd, stats_ref, kv, dq, dkv, kt, stat, *scratch):
    kt[...] = kv[:, :HEAD_DIM].T
    logsum, delta, unused = combine(stats_ref[:, :8, :], stats_ref[:, 8:, :])
    stat[:8, :] = logsum * LOG2E
    stat[8:, :] = delta
    dkv[...] = jnp.zeros_like(dkv)

    def rows(p):
        return rows_of(qd[p, :, :ROWS]), rows_of(qd[p, :, ROWS:])

    def products(p, score, dprob):
        q4, d4 = rows(p)
        score[...] = dot(kv[:, :HEAD_DIM], q4, NT)
        dprob[...] = dot(kv[:, HEAD_DIM:], d4, NT)

    def gradients(p, score, dprob, weight, dscore):
        base = stat[pl.ds(p, 1), :]
        delta = stat[pl.ds(8 + p, 1), :]
        for tile in tiles(KEYS):
            prob = jnp.exp2(score[tile, :] * (SCALE * LOG2E) - base)
            weight[tile, :] = prob.astype(BF16)
            dscore[tile, :] = (prob * (dprob[tile, :] - delta)).astype(BF16)
        q4, d4 = rows(p)
        dkv[:, HEAD_DIM:] += dot(weight[...], d4)
        dkv[:, :HEAD_DIM] += dot(dscore[...], q4)
        dq[p] = (dot(kt[...], dscore[...]) * SCALE).astype(BF16)

    def block(i, carry):
        for n in range(2):
            products(2 * i + n, *scratch[4 * n : 4 * n + 2])
        for n in range(2):
            gradients(2 * i + n, *scratch[4 * n : 4 * n + 4])
        return carry

    lax.fori_loop(0, GROUP // 2, block, 0)
    dkv[:, :HEAD_DIM] = dkv[:, :HEAD_DIM] * SCALE


def output_kernel(place, parts, stats_ref, upstream_ref, mixed_ref, keep_ref, give_ref):
    mine = place[1]
    unused, unused, weights = combine(
        stats_ref[:, pl.ds(mine, 1), :], stats_ref[:, pl.ds(8 + mine, 1), :]
    )
    mixed_t = jnp.sum(weights * parts[...].astype(F32), axis=0)
    heads_t = [mixed_t[:, h * POS : (h + 1) * POS] for h in range(HEADS)]
    mixed_ref[...] = jnp.concatenate([m.T for m in heads_t], axis=1).astype(BF16)
    mixed_rows = jnp.concatenate(heads_t, axis=0).astype(BF16)
    half = upstream_ref.shape[1] // 2
    first = place[0] == 0
    low, high = upstream_ref[:, :half], upstream_ref[:, half:]
    keep_ref[...] = dot(mixed_rows, jnp.where(first, low, high)).astype(BF16)
    give_ref[...] = dot(mixed_rows, jnp.where(first, high, low)).astype(BF16)


def attended_kernel(tokens_ref, mixed_ref, w_out_ref, attended_ref):
    attended_ref[...] = (
        tokens_ref[...].astype(F32) + dot(mixed_ref[...], w_out_ref[...])
    ).astype(BF16)


def input_kernel(place, dq_ref, dkv_ref, both_ref, keep_ref, give_ref):
    dq_t = jnp.sum(dq_ref[...].astype(F32), axis=0)
    dquery = jnp.concatenate(
        [dq_t[:, h * POS : (h + 1) * POS].T for h in range(HEADS)], axis=1
    ).astype(BF16)
    dkeyval = dkv_ref[...].astype(BF16)
    both_ref[:, :ROWS] = dquery
    both_ref[:, ROWS:] = dkeyval
    first = place[0] == 0
    low = jnp.concatenate([dquery[:, :256], dkeyval[:, :128]], axis=1)
    high = jnp.concatenate([dquery[:, 256:], dkeyval[:, 128:]], axis=1)
    keep_ref[...] = jnp.where(first, low, high)
    give_ref[...] = jnp.where(first, high, low)


def term_kernel(tokens_ref, other_ref, keep_ref, got_ref, term_ref):
    tokens = jnp.concatenate([tokens_ref[...], other_ref[...]], axis=0)
    grads = jnp.concatenate([keep_ref[...], got_ref[...]], axis=0)
    term_ref[...] = dot(tokens, grads, TN).astype(BF16)


def tokens_kernel(both_ref, w_query_ref, w_keyval_ref, grad_ref):
    grad_ref[...] = (
        dot(both_ref[:, :ROWS], w_query_ref[...], NT)
        + dot(both_ref[:, ROWS:], w_keyval_ref[...], NT)
    ).astype(BF16)


def plus(a, b):
    return (a.astype(F32) + b.astype(F32)).astype(BF16)


VM = pl.BlockSpec(memory_space=pltpu.VMEM)
SM = pl.BlockSpec(memory_space=pltpu.SMEM)


def call(kernel, ins, outs, in_specs, out_specs, scratch, flops):
    return pl.pallas_call(
        kernel,
        out_shape=outs,
        in_specs=in_specs,
        out_specs=out_specs,
        scratch_shapes=scratch,
        compiler_params=pltpu.CompilerParams(vmem_limit_bytes=VMEM_LIMIT),
        cost_estimate=pl.CostEstimate(flops=flops, bytes_accessed=6_000_000 if flops else 0, transcendentals=0),
    )(*ins)


def shape(*dims, dtype=BF16):
    return jax.ShapeDtypeStruct(dims, dtype)


def swap(blocks, axes):
    return lax.all_to_all(blocks, axes, 0, 0)


def share(array, axes, count):
    return swap(jnp.broadcast_to(array[None], (count,) + array.shape), axes)


def added(blocks):
    return jnp.sum(blocks.astype(F32), axis=0)


def body(tokens, upstream, w_query, w_keyval, w_out):
    local = tokens[0]
    cotangent = upstream[0]
    core = lax.axis_index("core")
    group = lax.axis_index("x") * 2 + lax.axis_index("yl")
    place = jnp.stack([core, group]).astype(jnp.int32)
    query = jnp.dot(local, w_query, preferred_element_type=F32).astype(BF16)
    dmixed = jnp.dot(cotangent, w_out.T, preferred_element_type=F32).astype(BF16)
    qd = jnp.concatenate([query, dmixed], axis=1)
    qds = share(qd, ("x", "yl"), 8)
    qd, early = lax.optimization_barrier((qd, local))
    keyval = jnp.dot(early, w_keyval, preferred_element_type=F32).astype(BF16)
    kvs = lax.all_gather(keyval, "z", axis=0, tiled=True)
    tokens_other = send(early, "core", 2, 1)
    kvs, tokens_other, place = lax.optimization_barrier((kvs, tokens_other, place))

    mixed_parts, stats = call(
        forward_kernel,
        [qds, kvs],
        [shape(8, HEAD_DIM, ROWS), shape(8, 16, ROWS, dtype=F32)],
        [VM] * 2,
        [VM] * 2,
        [
            pltpu.VMEM((HEAD_DIM, KEYS), BF16),
            pltpu.VMEM((16, ROWS), F32),
            pltpu.VMEM((KEYS, ROWS), F32),
            pltpu.VMEM((KEYS, ROWS), F32),
            pltpu.VMEM((KEYS, ROWS), BF16),
            pltpu.VMEM((KEYS, ROWS), BF16),
        ],
        10_000_000_000,
    )
    all_stats = swap(stats, ("x", "yl"))
    mixed_parts, all_stats = lax.optimization_barrier((mixed_parts, all_stats))
    mine = swap(mixed_parts, ("x", "yl"))
    dq_parts, dkv_parts = call(
        backward_kernel,
        [qds, all_stats, kvs],
        [shape(8, HEAD_DIM, ROWS), shape(KEYS, 2 * HEAD_DIM, dtype=F32)],
        [VM] * 3,
        [VM] * 2,
        [
            pltpu.VMEM((HEAD_DIM, KEYS), BF16),
            pltpu.VMEM((16, ROWS), F32),
        ]
        + [pltpu.VMEM((KEYS, ROWS), t) for t in (F32, F32, BF16, BF16)] * 2,
        16_000_000_000,
    )
    dq_parts, mine = lax.optimization_barrier((dq_parts, mine))
    dkv = lax.psum_scatter(dkv_parts, "z", scatter_dimension=0, tiled=True)
    mixed, keep_o, give_o = call(
        output_kernel,
        [place, mine, all_stats, cotangent],
        [shape(POS, ROWS), shape(512, 768), shape(512, 768)],
        [SM] + [VM] * 3,
        [VM] * 3,
        [],
        400_000_000,
    )
    term_o = plus(keep_o, send(give_o, "core", 2, 1))
    attended = call(
        attended_kernel,
        [local, mixed, w_out],
        shape(*local.shape),
        [VM] * 3,
        VM,
        [],
        20_000_000_000,
    )
    term_o, attended, dq_parts = lax.optimization_barrier((term_o, attended, dq_parts))
    dqs = swap(dq_parts, ("x", "yl"))
    dqs, term_o = lax.optimization_barrier((dqs, term_o))
    term_o = swap(term_o.reshape(4, 128, 768), "x")

    both, keep_i, give_i = call(
        input_kernel,
        [place, dqs, dkv],
        [shape(POS, 768), shape(POS, 384), shape(POS, 384)],
        [SM] + [VM] * 2,
        [VM] * 3,
        [],
        0,
    )
    term_i = call(
        term_kernel,
        [local, tokens_other, keep_i, send(give_i, "core", 2, 1)],
        shape(1536, 384),
        [VM] * 4,
        VM,
        [],
        0,
    )
    term_i, term_o = lax.optimization_barrier((term_i, term_o))
    grad_tokens = call(
        tokens_kernel,
        [both, w_query, w_keyval],
        shape(*local.shape),
        [VM] * 3,
        VM,
        [],
        300_000_000,
    )
    yl, yh = lax.axis_index("yl"), lax.axis_index("yh")
    blocks = added(term_o).astype(BF16).reshape(8, 2, 8, 2, 384)
    blocks = blocks.transpose(1, 3, 0, 2, 4).reshape(4, 64, 384)

    def block(step_l, step_h):
        at = (yl + step_l) % 2 * 2 + (yh + step_h) % 2
        return lax.dynamic_index_in_dim(blocks, at, 0, keepdims=False)

    steps = [(0, 1), (1, 0), (1, 1)]
    term_o = block(0, 0).astype(F32)
    term_o = term_o + sum(send_y(block(*step), *step).astype(F32) for step in steps)
    term_i = swap(term_i.reshape(4, 384, 384), "x")
    grad_tokens, term_i, term_o = lax.optimization_barrier((grad_tokens, term_i, term_o))
    term_i = added(term_i).reshape(8, 2, 24, 384)
    here = (jnp.arange(2) == lax.axis_index("yl"))[None, :, None, None]
    term_o = jnp.where(here, term_o.reshape(8, 1, 8, 384), 0.0)
    ends = jnp.concatenate([term_i, term_o], axis=2).astype(BF16).reshape(16, 32, 384)
    ends = added(swap(ends, ("z", "yl")))
    got = send(ends, "yh", 2, 1)
    ends = jnp.concatenate(
        [
            ends[:24] + got[:24],
            jnp.where(yh == 0, ends[24:], got[24:]),
            jnp.where(yh == 0, got[24:], ends[24:]),
        ]
    )
    other = send(ends, "core", 2, 1)
    low, high = jnp.where(core == 0, ends, other), jnp.where(core == 0, other, ends)
    grad_o = jnp.concatenate([low[24:32], low[32:], high[24:32], high[32:]], axis=1)
    return (
        attended[None],
        grad_tokens[None],
        jnp.concatenate([low[:24, :256], high[:24, :256]], axis=1),
        jnp.concatenate([low[:24, 256:], high[:24, 256:]], axis=1),
        grad_o,
    )


def solution(mesh):
    torus = Mesh(mesh.devices.reshape(4, 8, 2, 2, 2), AXES)
    return jax.shard_map(
        body,
        mesh=torus,
        in_specs=(P(DP, SEQ, None), P(DP, SEQ, None), P(), P(), P()),
        out_specs=(
            P(DP, SEQ, None),
            P(DP, SEQ, None),
            P(SEQ, None),
            P(SEQ, None),
            P(SEQ, None),
        ),
        check_vma=False,
    )
```

```python
import math

import jax
import jax.numpy as jnp
from jax import lax
from jax.experimental import pallas as pl
from jax.experimental.pallas import tpu as pltpu
from jax.sharding import Mesh, PartitionSpec as P

HEADS = 4
HEAD_DIM = 128
POS = 128
ROWS = HEADS * POS
GROUP = 8
KEYS = 8 * POS
TILE = 16
SCALE = 1.0 / HEAD_DIM**0.5
LOG2E = math.log2(math.e)
AXES = ("x", "z", "yl", "yh", "core")
SEQ = ("x", "z", "yl")
DP = ("yh", "core")
NT = (((1,), (1,)), ((), ()))
TN = (((0,), (0,)), ((), ()))
F32 = jnp.float32
BF16 = jnp.bfloat16
VMEM_LIMIT = 56 * 1024 * 1024


def dot(a, b, dims=(((1,), (0,)), ((), ()))):
    return lax.dot_general(a, b, dims, preferred_element_type=F32)


def send(array, axis, size, step):
    return lax.ppermute(array, axis, [(i, (i + step) % size) for i in range(size)])


def send_y(array, step_l, step_h):
    pairs = [
        (a * 2 + b, (a + step_l) % 2 * 2 + (b + step_h) % 2) for a in range(2) for b in range(2)
    ]
    return lax.ppermute(array, ("yl", "yh"), pairs)


def rows_of(block):
    return jnp.concatenate(
        [block[:, h * HEAD_DIM : (h + 1) * HEAD_DIM] for h in range(HEADS)], axis=0
    )


def tiles(count):
    return [slice(t * TILE, (t + 1) * TILE) for t in range(count // TILE)]


def fold(values, op):
    return op(values.reshape(-1, 8, values.shape[1]), axis=0)


def forward_kernel(qd, kv, mixed, stats_out, vt, stats_ref, *scratch):
    vt[...] = kv[:, HEAD_DIM:].T

    def scores(p, score):
        score[...] = dot(kv[:, :HEAD_DIM], rows_of(qd[p, :, :ROWS]), NT)

    def softmax(p, score, weight):
        top = jnp.full((8, ROWS), -jnp.inf, F32)
        for part in tiles(KEYS):
            top = jnp.maximum(top, fold(score[part, :], jnp.max))
        top = jnp.max(top, axis=0, keepdims=True)
        base = top * (SCALE * LOG2E)
        total = jnp.zeros((8, ROWS), F32)
        for part in tiles(KEYS):
            e = jnp.exp2(score[part, :] * (SCALE * LOG2E) - base)
            total = total + fold(e, jnp.sum)
            weight[part, :] = e.astype(BF16)
        total = jnp.sum(total, axis=0, keepdims=True)
        acc = dot(vt[...], weight[...]) * (1.0 / total)
        mixed[p] = acc.astype(BF16)
        stats_ref[pl.ds(p, 1), :] = top * SCALE + jnp.log(total)
        d4 = rows_of(qd[p, :, ROWS:])
        stats_ref[pl.ds(8 + p, 1), :] = jnp.sum(acc * d4.T.astype(F32), axis=0, keepdims=True)

    def block(i, carry):
        for n in range(2):
            scores(2 * i + n, scratch[n])
        for n in range(2):
            softmax(2 * i + n, scratch[n], scratch[2 + n])
        return carry

    lax.fori_loop(0, GROUP // 2, block, 0)
    for i in range(GROUP):
        stats_out[i] = stats_ref[...]


def combine(logs, bars):
    top = jnp.max(logs, axis=0)
    weights = jnp.exp(logs - top)
    total = jnp.sum(weights, axis=0)
    weights = weights / total
    return top + jnp.log(total), jnp.sum(weights * bars, axis=0), weights


def backward_kernel(qd, stats_ref, kv, dq, dkv_out, kt, stat, dkv, *scratch):
    kt[...] = kv[:, :HEAD_DIM].T
    logsum, delta, unused = combine(stats_ref[:, :8, :], stats_ref[:, 8:, :])
    stat[:8, :] = logsum * LOG2E
    stat[8:, :] = delta
    dkv[...] = jnp.zeros_like(dkv)

    def rows(p):
        return rows_of(qd[p, :, :ROWS]), rows_of(qd[p, :, ROWS:])

    def products(p, score, dprob):
        q4, d4 = rows(p)
        score[...] = dot(kv[:, :HEAD_DIM], q4, NT)
        dprob[...] = dot(kv[:, HEAD_DIM:], d4, NT)

    def gradients(p, score, dprob, weight, dscore):
        base = stat[pl.ds(p, 1), :]
        delta = stat[pl.ds(8 + p, 1), :]
        for tile in tiles(KEYS):
            prob = jnp.exp2(score[tile, :] * (SCALE * LOG2E) - base)
            weight[tile, :] = prob.astype(BF16)
            dscore[tile, :] = (prob * (dprob[tile, :] - delta)).astype(BF16)
        q4, d4 = rows(p)
        dkv[:, HEAD_DIM:] += dot(weight[...], d4)
        dkv[:, :HEAD_DIM] += dot(dscore[...], q4)
        dq[p] = (dot(kt[...], dscore[...]) * SCALE).astype(BF16)

    def block(i, carry):
        for n in range(2):
            products(2 * i + n, *scratch[4 * n : 4 * n + 2])
        for n in range(2):
            gradients(2 * i + n, *scratch[4 * n : 4 * n + 4])
        return carry

    lax.fori_loop(0, GROUP // 2, block, 0)
    dkv_out[:, :HEAD_DIM] = (dkv[:, :HEAD_DIM] * SCALE).astype(BF16)
    dkv_out[:, HEAD_DIM:] = dkv[:, HEAD_DIM:].astype(BF16)


def output_kernel(place, parts, stats_ref, upstream_ref, mixed_ref, keep_ref, give_ref):
    mine = place[1]
    unused, unused, weights = combine(
        stats_ref[:, pl.ds(mine, 1), :], stats_ref[:, pl.ds(8 + mine, 1), :]
    )
    mixed_t = jnp.sum(weights * parts[...].astype(F32), axis=0)
    heads_t = [mixed_t[:, h * POS : (h + 1) * POS] for h in range(HEADS)]
    mixed_ref[...] = jnp.concatenate([m.T for m in heads_t], axis=1).astype(BF16)
    mixed_rows = jnp.concatenate(heads_t, axis=0).astype(BF16)
    half = upstream_ref.shape[1] // 2
    first = place[0] == 0
    low, high = upstream_ref[:, :half], upstream_ref[:, half:]
    keep_ref[...] = dot(mixed_rows, jnp.where(first, low, high)).astype(BF16)
    give_ref[...] = dot(mixed_rows, jnp.where(first, high, low)).astype(BF16)


def attended_kernel(tokens_ref, mixed_ref, w_out_ref, attended_ref):
    attended_ref[...] = (
        tokens_ref[...].astype(F32) + dot(mixed_ref[...], w_out_ref[...])
    ).astype(BF16)


def input_kernel(place, dq_ref, dkv_ref, both_ref, keep_ref, give_ref):
    dq_t = jnp.sum(dq_ref[...].astype(F32), axis=0)
    dquery = jnp.concatenate(
        [dq_t[:, h * POS : (h + 1) * POS].T for h in range(HEADS)], axis=1
    ).astype(BF16)
    dkeyval = dkv_ref[...].astype(BF16)
    both_ref[:, :ROWS] = dquery
    both_ref[:, ROWS:] = dkeyval
    first = place[0] == 0
    low = jnp.concatenate([dquery[:, :256], dkeyval[:, :128]], axis=1)
    high = jnp.concatenate([dquery[:, 256:], dkeyval[:, 128:]], axis=1)
    keep_ref[...] = jnp.where(first, low, high)
    give_ref[...] = jnp.where(first, high, low)


def term_kernel(tokens_ref, other_ref, keep_ref, got_ref, term_ref):
    tokens = jnp.concatenate([tokens_ref[...], other_ref[...]], axis=0)
    grads = jnp.concatenate([keep_ref[...], got_ref[...]], axis=0)
    term_ref[...] = dot(tokens, grads, TN).astype(BF16)


def tokens_kernel(both_ref, w_query_ref, w_keyval_ref, grad_ref):
    grad_ref[...] = (
        dot(both_ref[:, :ROWS], w_query_ref[...], NT)
        + dot(both_ref[:, ROWS:], w_keyval_ref[...], NT)
    ).astype(BF16)


def plus(a, b):
    return (a.astype(F32) + b.astype(F32)).astype(BF16)


VM = pl.BlockSpec(memory_space=pltpu.VMEM)
SM = pl.BlockSpec(memory_space=pltpu.SMEM)


def call(kernel, ins, outs, in_specs, out_specs, scratch, flops):
    return pl.pallas_call(
        kernel,
        out_shape=outs,
        in_specs=in_specs,
        out_specs=out_specs,
        scratch_shapes=scratch,
        compiler_params=pltpu.CompilerParams(vmem_limit_bytes=VMEM_LIMIT),
        cost_estimate=pl.CostEstimate(flops=flops, bytes_accessed=6_000_000 if flops else 0, transcendentals=0),
    )(*ins)


def shape(*dims, dtype=BF16):
    return jax.ShapeDtypeStruct(dims, dtype)


def swap(blocks, axes):
    return lax.all_to_all(blocks, axes, 0, 0)


def share(array, axes, count):
    return swap(jnp.broadcast_to(array[None], (count,) + array.shape), axes)


def added(blocks):
    return jnp.sum(blocks.astype(F32), axis=0)


def body(tokens, upstream, w_query, w_keyval, w_out):
    local = tokens[0]
    cotangent = upstream[0]
    core = lax.axis_index("core")
    group = lax.axis_index("x") * 2 + lax.axis_index("yl")
    place = jnp.stack([core, group]).astype(jnp.int32)
    query = jnp.dot(local, w_query, preferred_element_type=F32).astype(BF16)
    dmixed = jnp.dot(cotangent, w_out.T, preferred_element_type=F32).astype(BF16)
    qd = jnp.concatenate([query, dmixed], axis=1)
    qds = share(qd, ("x", "yl"), 8)
    qd, early = lax.optimization_barrier((qd, local))
    keyval = jnp.dot(early, w_keyval, preferred_element_type=F32).astype(BF16)
    kvs = lax.all_gather(keyval, "z", axis=0, tiled=True)
    tokens_other = send(early, "core", 2, 1)
    kvs, tokens_other, place = lax.optimization_barrier((kvs, tokens_other, place))

    mixed_parts, stats = call(
        forward_kernel,
        [qds, kvs],
        [shape(8, HEAD_DIM, ROWS), shape(8, 16, ROWS, dtype=F32)],
        [VM] * 2,
        [VM] * 2,
        [
            pltpu.VMEM((HEAD_DIM, KEYS), BF16),
            pltpu.VMEM((16, ROWS), F32),
            pltpu.VMEM((KEYS, ROWS), F32),
            pltpu.VMEM((KEYS, ROWS), F32),
            pltpu.VMEM((KEYS, ROWS), BF16),
            pltpu.VMEM((KEYS, ROWS), BF16),
        ],
        10_000_000_000,
    )
    all_stats = swap(stats, ("x", "yl"))
    mixed_parts, all_stats = lax.optimization_barrier((mixed_parts, all_stats))
    mine = swap(mixed_parts, ("x", "yl"))
    dq_parts, dkv_parts = call(
        backward_kernel,
        [qds, all_stats, kvs],
        [shape(8, HEAD_DIM, ROWS), shape(KEYS, 2 * HEAD_DIM)],
        [VM] * 3,
        [VM] * 2,
        [
            pltpu.VMEM((HEAD_DIM, KEYS), BF16),
            pltpu.VMEM((16, ROWS), F32),
            pltpu.VMEM((KEYS, 2 * HEAD_DIM), F32),
        ]
        + [pltpu.VMEM((KEYS, ROWS), t) for t in (F32, F32, BF16, BF16)] * 2,
        16_000_000_000,
    )
    dq_parts, mine = lax.optimization_barrier((dq_parts, mine))
    dkv = lax.psum_scatter(dkv_parts, "z", scatter_dimension=0, tiled=True)
    mixed, keep_o, give_o = call(
        output_kernel,
        [place, mine, all_stats, cotangent],
        [shape(POS, ROWS), shape(512, 768), shape(512, 768)],
        [SM] + [VM] * 3,
        [VM] * 3,
        [],
        400_000_000,
    )
    term_o = plus(keep_o, send(give_o, "core", 2, 1))
    attended = call(
        attended_kernel,
        [local, mixed, w_out],
        shape(*local.shape),
        [VM] * 3,
        VM,
        [],
        20_000_000_000,
    )
    term_o, attended, dq_parts = lax.optimization_barrier((term_o, attended, dq_parts))
    dqs = swap(dq_parts, ("x", "yl"))
    dqs, term_o = lax.optimization_barrier((dqs, term_o))
    term_o = swap(term_o.reshape(4, 128, 768), "x")

    both, keep_i, give_i = call(
        input_kernel,
        [place, dqs, dkv],
        [shape(POS, 768), shape(POS, 384), shape(POS, 384)],
        [SM] + [VM] * 2,
        [VM] * 3,
        [],
        0,
    )
    term_i = call(
        term_kernel,
        [local, tokens_other, keep_i, send(give_i, "core", 2, 1)],
        shape(1536, 384),
        [VM] * 4,
        VM,
        [],
        0,
    )
    term_i, term_o = lax.optimization_barrier((term_i, term_o))
    grad_tokens = call(
        tokens_kernel,
        [both, w_query, w_keyval],
        shape(*local.shape),
        [VM] * 3,
        VM,
        [],
        300_000_000,
    )
    yl, yh = lax.axis_index("yl"), lax.axis_index("yh")
    blocks = added(term_o).astype(BF16).reshape(8, 2, 8, 2, 384)
    blocks = blocks.transpose(1, 3, 0, 2, 4).reshape(4, 64, 384)

    def block(step_l, step_h):
        at = (yl + step_l) % 2 * 2 + (yh + step_h) % 2
        return lax.dynamic_index_in_dim(blocks, at, 0, keepdims=False)

    steps = [(0, 1), (1, 0), (1, 1)]
    term_o = block(0, 0).astype(F32)
    term_o = term_o + sum(send_y(block(*step), *step).astype(F32) for step in steps)
    term_i = swap(term_i.reshape(4, 384, 384), "x")
    grad_tokens, term_i, term_o = lax.optimization_barrier((grad_tokens, term_i, term_o))
    term_i = added(term_i).reshape(8, 2, 24, 384)
    here = (jnp.arange(2) == lax.axis_index("yl"))[None, :, None, None]
    term_o = jnp.where(here, term_o.reshape(8, 1, 8, 384), 0.0)
    ends = jnp.concatenate([term_i, term_o], axis=2).astype(BF16).reshape(16, 32, 384)
    ends = added(swap(ends, ("z", "yl")))
    got = send(ends, "yh", 2, 1)
    ends = jnp.concatenate(
        [
            ends[:24] + got[:24],
            jnp.where(yh == 0, ends[24:], got[24:]),
            jnp.where(yh == 0, got[24:], ends[24:]),
        ]
    )
    other = send(ends, "core", 2, 1)
    low, high = jnp.where(core == 0, ends, other), jnp.where(core == 0, other, ends)
    grad_o = jnp.concatenate([low[24:32], low[32:], high[24:32], high[32:]], axis=1)
    return (
        attended[None],
        grad_tokens[None],
        jnp.concatenate([low[:24, :256], high[:24, :256]], axis=1),
        jnp.concatenate([low[:24, 256:], high[:24, 256:]], axis=1),
        grad_o,
    )


def solution(mesh):
    torus = Mesh(mesh.devices.reshape(4, 8, 2, 2, 2), AXES)
    return jax.shard_map(
        body,
        mesh=torus,
        in_specs=(P(DP, SEQ, None), P(DP, SEQ, None), P(), P(), P()),
        out_specs=(
            P(DP, SEQ, None),
            P(DP, SEQ, None),
            P(SEQ, None),
            P(SEQ, None),
            P(SEQ, None),
        ),
        check_vma=False,
    )
```

```python
import math

import jax
import jax.numpy as jnp
from jax import lax
from jax.experimental import pallas as pl
from jax.experimental.pallas import tpu as pltpu
from jax.sharding import Mesh, PartitionSpec as P

HEADS = 4
HEAD_DIM = 128
POS = 128
ROWS = HEADS * POS
GROUP = 8
KEYS = 8 * POS
TILE = 16
SCALE = 1.0 / HEAD_DIM**0.5
LOG2E = math.log2(math.e)
AXES = ("x", "z", "yl", "yh", "core")
SEQ = ("x", "z", "yl")
DP = ("yh", "core")
NT = (((1,), (1,)), ((), ()))
TN = (((0,), (0,)), ((), ()))
F32 = jnp.float32
BF16 = jnp.bfloat16
VMEM_LIMIT = 56 * 1024 * 1024


def dot(a, b, dims=(((1,), (0,)), ((), ()))):
    return lax.dot_general(a, b, dims, preferred_element_type=F32)


def send(array, axis, size, step):
    return lax.ppermute(array, axis, [(i, (i + step) % size) for i in range(size)])


def send_y(array, step_l, step_h):
    pairs = [
        (a * 2 + b, (a + step_l) % 2 * 2 + (b + step_h) % 2) for a in range(2) for b in range(2)
    ]
    return lax.ppermute(array, ("yl", "yh"), pairs)


def rows_of(block):
    return jnp.concatenate(
        [block[:, h * HEAD_DIM : (h + 1) * HEAD_DIM] for h in range(HEADS)], axis=0
    )


def tiles(count):
    return [slice(t * TILE, (t + 1) * TILE) for t in range(count // TILE)]


def fold(values, op):
    return op(values.reshape(-1, 8, values.shape[1]), axis=0)


def project_kernel(tokens_ref, upstream_ref, w_query_ref, w_out_ref, out_ref):
    query = dot(tokens_ref[...], w_query_ref[...]).astype(BF16)
    dmixed = dot(upstream_ref[...], w_out_ref[...], NT).astype(BF16)
    for i in range(GROUP):
        out_ref[i, :, :ROWS] = query
        out_ref[i, :, ROWS:] = dmixed


def forward_kernel(qd, kv, mixed, stats_out, vt, stats_ref, *scratch):
    vt[...] = kv[:, HEAD_DIM:].T

    def scores(p, score):
        score[...] = dot(kv[:, :HEAD_DIM], rows_of(qd[p, :, :ROWS]), NT)

    def softmax(p, score, weight):
        top = jnp.full((8, ROWS), -jnp.inf, F32)
        for part in tiles(KEYS):
            top = jnp.maximum(top, fold(score[part, :], jnp.max))
        top = jnp.max(top, axis=0, keepdims=True)
        base = top * (SCALE * LOG2E)
        total = jnp.zeros((8, ROWS), F32)
        for part in tiles(KEYS):
            e = jnp.exp2(score[part, :] * (SCALE * LOG2E) - base)
            total = total + fold(e, jnp.sum)
            weight[part, :] = e.astype(BF16)
        total = jnp.sum(total, axis=0, keepdims=True)
        acc = dot(vt[...], weight[...]) * (1.0 / total)
        mixed[p] = acc.astype(BF16)
        stats_ref[pl.ds(p, 1), :] = top * SCALE + jnp.log(total)
        d4 = rows_of(qd[p, :, ROWS:])
        stats_ref[pl.ds(8 + p, 1), :] = jnp.sum(acc * d4.T.astype(F32), axis=0, keepdims=True)

    def block(i, carry):
        for n in range(2):
            scores(2 * i + n, scratch[n])
        for n in range(2):
            softmax(2 * i + n, scratch[n], scratch[2 + n])
        return carry

    lax.fori_loop(0, GROUP // 2, block, 0)
    for i in range(GROUP):
        stats_out[i] = stats_ref[...]


def combine(logs, bars):
    top = jnp.max(logs, axis=0)
    weights = jnp.exp(logs - top)
    total = jnp.sum(weights, axis=0)
    weights = weights / total
    return top + jnp.log(total), jnp.sum(weights * bars, axis=0), weights


def backward_kernel(qd, stats_ref, kv, dq, dkv, kt, stat, *scratch):
    kt[...] = kv[:, :HEAD_DIM].T
    logsum, delta, unused = combine(stats_ref[:, :8, :], stats_ref[:, 8:, :])
    stat[:8, :] = logsum * LOG2E
    stat[8:, :] = delta
    dkv[...] = jnp.zeros_like(dkv)

    def rows(p):
        return rows_of(qd[p, :, :ROWS]), rows_of(qd[p, :, ROWS:])

    def products(p, score, dprob):
        q4, d4 = rows(p)
        score[...] = dot(kv[:, :HEAD_DIM], q4, NT)
        dprob[...] = dot(kv[:, HEAD_DIM:], d4, NT)

    def gradients(p, score, dprob, weight, dscore):
        base = stat[pl.ds(p, 1), :]
        delta = stat[pl.ds(8 + p, 1), :]
        for tile in tiles(KEYS):
            prob = jnp.exp2(score[tile, :] * (SCALE * LOG2E) - base)
            weight[tile, :] = prob.astype(BF16)
            dscore[tile, :] = (prob * (dprob[tile, :] - delta)).astype(BF16)
        q4, d4 = rows(p)
        dkv[:, HEAD_DIM:] += dot(weight[...], d4)
        dkv[:, :HEAD_DIM] += dot(dscore[...], q4)
        dq[p] = (dot(kt[...], dscore[...]) * SCALE).astype(BF16)

    def block(i, carry):
        for n in range(2):
            products(2 * i + n, *scratch[4 * n : 4 * n + 2])
        for n in range(2):
            gradients(2 * i + n, *scratch[4 * n : 4 * n + 4])
        return carry

    lax.fori_loop(0, GROUP // 2, block, 0)
    dkv[:, :HEAD_DIM] = dkv[:, :HEAD_DIM] * SCALE


def output_kernel(place, parts, stats_ref, upstream_ref, mixed_ref, keep_ref, give_ref):
    mine = place[1]
    unused, unused, weights = combine(
        stats_ref[:, pl.ds(mine, 1), :], stats_ref[:, pl.ds(8 + mine, 1), :]
    )
    mixed_t = jnp.sum(weights * parts[...].astype(F32), axis=0)
    heads_t = [mixed_t[:, h * POS : (h + 1) * POS] for h in range(HEADS)]
    mixed_ref[...] = jnp.concatenate([m.T for m in heads_t], axis=1).astype(BF16)
    mixed_rows = jnp.concatenate(heads_t, axis=0).astype(BF16)
    half = upstream_ref.shape[1] // 2
    first = place[0] == 0
    low, high = upstream_ref[:, :half], upstream_ref[:, half:]
    keep_ref[...] = dot(mixed_rows, jnp.where(first, low, high)).astype(BF16)
    give_ref[...] = dot(mixed_rows, jnp.where(first, high, low)).astype(BF16)


def attended_kernel(tokens_ref, mixed_ref, w_out_ref, attended_ref):
    attended_ref[...] = (
        tokens_ref[...].astype(F32) + dot(mixed_ref[...], w_out_ref[...])
    ).astype(BF16)


def input_kernel(place, dq_ref, dkv_ref, both_ref, keep_ref, give_ref):
    dq_t = jnp.sum(dq_ref[...].astype(F32), axis=0)
    dquery = jnp.concatenate(
        [dq_t[:, h * POS : (h + 1) * POS].T for h in range(HEADS)], axis=1
    ).astype(BF16)
    dkeyval = dkv_ref[...].astype(BF16)
    both_ref[:, :ROWS] = dquery
    both_ref[:, ROWS:] = dkeyval
    first = place[0] == 0
    low = jnp.concatenate([dquery[:, :256], dkeyval[:, :128]], axis=1)
    high = jnp.concatenate([dquery[:, 256:], dkeyval[:, 128:]], axis=1)
    keep_ref[...] = jnp.where(first, low, high)
    give_ref[...] = jnp.where(first, high, low)


def term_kernel(tokens_ref, other_ref, keep_ref, got_ref, term_ref):
    tokens = jnp.concatenate([tokens_ref[...], other_ref[...]], axis=0)
    grads = jnp.concatenate([keep_ref[...], got_ref[...]], axis=0)
    term_ref[...] = dot(tokens, grads, TN).astype(BF16)


def tokens_kernel(both_ref, w_query_ref, w_keyval_ref, grad_ref):
    grad_ref[...] = (
        dot(both_ref[:, :ROWS], w_query_ref[...], NT)
        + dot(both_ref[:, ROWS:], w_keyval_ref[...], NT)
    ).astype(BF16)


def plus(a, b):
    return (a.astype(F32) + b.astype(F32)).astype(BF16)


VM = pl.BlockSpec(memory_space=pltpu.VMEM)
SM = pl.BlockSpec(memory_space=pltpu.SMEM)


def call(kernel, ins, outs, in_specs, out_specs, scratch, flops):
    return pl.pallas_call(
        kernel,
        out_shape=outs,
        in_specs=in_specs,
        out_specs=out_specs,
        scratch_shapes=scratch,
        compiler_params=pltpu.CompilerParams(vmem_limit_bytes=VMEM_LIMIT),
        cost_estimate=pl.CostEstimate(flops=flops, bytes_accessed=6_000_000 if flops else 0, transcendentals=0),
    )(*ins)


def shape(*dims, dtype=BF16):
    return jax.ShapeDtypeStruct(dims, dtype)


def swap(blocks, axes):
    return lax.all_to_all(blocks, axes, 0, 0)


def added(blocks):
    return jnp.sum(blocks.astype(F32), axis=0)


def body(tokens, upstream, w_query, w_keyval, w_out):
    local = tokens[0]
    cotangent = upstream[0]
    core = lax.axis_index("core")
    group = lax.axis_index("x") * 2 + lax.axis_index("yl")
    place = jnp.stack([core, group]).astype(jnp.int32)
    copies = call(
        project_kernel,
        [local, cotangent, w_query, w_out],
        shape(8, POS, 2 * ROWS),
        [VM] * 4,
        VM,
        [],
        400_000_000,
    )
    qds = swap(copies, ("x", "yl"))
    copies, early = lax.optimization_barrier((copies, local))
    keyval = jnp.dot(early, w_keyval, preferred_element_type=F32).astype(BF16)
    kvs = lax.all_gather(keyval, "z", axis=0, tiled=True)
    tokens_other = send(early, "core", 2, 1)
    kvs, tokens_other, place = lax.optimization_barrier((kvs, tokens_other, place))

    mixed_parts, stats = call(
        forward_kernel,
        [qds, kvs],
        [shape(8, HEAD_DIM, ROWS), shape(8, 16, ROWS, dtype=F32)],
        [VM] * 2,
        [VM] * 2,
        [
            pltpu.VMEM((HEAD_DIM, KEYS), BF16),
            pltpu.VMEM((16, ROWS), F32),
            pltpu.VMEM((KEYS, ROWS), F32),
            pltpu.VMEM((KEYS, ROWS), F32),
            pltpu.VMEM((KEYS, ROWS), BF16),
            pltpu.VMEM((KEYS, ROWS), BF16),
        ],
        10_000_000_000,
    )
    all_stats = swap(stats, ("x", "yl"))
    mixed_parts, all_stats = lax.optimization_barrier((mixed_parts, all_stats))
    mine = swap(mixed_parts, ("x", "yl"))
    dq_parts, dkv_parts = call(
        backward_kernel,
        [qds, all_stats, kvs],
        [shape(8, HEAD_DIM, ROWS), shape(KEYS, 2 * HEAD_DIM, dtype=F32)],
        [VM] * 3,
        [VM] * 2,
        [
            pltpu.VMEM((HEAD_DIM, KEYS), BF16),
            pltpu.VMEM((16, ROWS), F32),
        ]
        + [pltpu.VMEM((KEYS, ROWS), t) for t in (F32, F32, BF16, BF16)] * 2,
        16_000_000_000,
    )
    dq_parts, mine = lax.optimization_barrier((dq_parts, mine))
    dkv = lax.psum_scatter(dkv_parts, "z", scatter_dimension=0, tiled=True)
    mixed, keep_o, give_o = call(
        output_kernel,
        [place, mine, all_stats, cotangent],
        [shape(POS, ROWS), shape(512, 768), shape(512, 768)],
        [SM] + [VM] * 3,
        [VM] * 3,
        [],
        400_000_000,
    )
    term_o = plus(keep_o, send(give_o, "core", 2, 1))
    attended = call(
        attended_kernel,
        [local, mixed, w_out],
        shape(*local.shape),
        [VM] * 3,
        VM,
        [],
        20_000_000_000,
    )
    term_o, attended, dq_parts = lax.optimization_barrier((term_o, attended, dq_parts))
    dqs = swap(dq_parts, ("x", "yl"))
    dqs, term_o = lax.optimization_barrier((dqs, term_o))
    term_o = swap(term_o.reshape(4, 128, 768), "x")

    both, keep_i, give_i = call(
        input_kernel,
        [place, dqs, dkv],
        [shape(POS, 768), shape(POS, 384), shape(POS, 384)],
        [SM] + [VM] * 2,
        [VM] * 3,
        [],
        0,
    )
    term_i = call(
        term_kernel,
        [local, tokens_other, keep_i, send(give_i, "core", 2, 1)],
        shape(1536, 384),
        [VM] * 4,
        VM,
        [],
        0,
    )
    term_i, term_o = lax.optimization_barrier((term_i, term_o))
    grad_tokens = call(
        tokens_kernel,
        [both, w_query, w_keyval],
        shape(*local.shape),
        [VM] * 3,
        VM,
        [],
        300_000_000,
    )
    yl, yh = lax.axis_index("yl"), lax.axis_index("yh")
    blocks = added(term_o).astype(BF16).reshape(8, 2, 8, 2, 384)
    blocks = blocks.transpose(1, 3, 0, 2, 4).reshape(4, 64, 384)

    def block(step_l, step_h):
        at = (yl + step_l) % 2 * 2 + (yh + step_h) % 2
        return lax.dynamic_index_in_dim(blocks, at, 0, keepdims=False)

    steps = [(0, 1), (1, 0), (1, 1)]
    term_o = block(0, 0).astype(F32)
    term_o = term_o + sum(send_y(block(*step), *step).astype(F32) for step in steps)
    term_i = swap(term_i.reshape(4, 384, 384), "x")
    grad_tokens, term_i, term_o = lax.optimization_barrier((grad_tokens, term_i, term_o))
    term_i = added(term_i).reshape(8, 2, 24, 384)
    here = (jnp.arange(2) == lax.axis_index("yl"))[None, :, None, None]
    term_o = jnp.where(here, term_o.reshape(8, 1, 8, 384), 0.0)
    ends = jnp.concatenate([term_i, term_o], axis=2).astype(BF16).reshape(16, 32, 384)
    ends = added(swap(ends, ("z", "yl")))
    got = send(ends, "yh", 2, 1)
    ends = jnp.concatenate(
        [
            ends[:24] + got[:24],
            jnp.where(yh == 0, ends[24:], got[24:]),
            jnp.where(yh == 0, got[24:], ends[24:]),
        ]
    )
    other = send(ends, "core", 2, 1)
    low, high = jnp.where(core == 0, ends, other), jnp.where(core == 0, other, ends)
    grad_o = jnp.concatenate([low[24:32], low[32:], high[24:32], high[32:]], axis=1)
    return (
        attended[None],
        grad_tokens[None],
        jnp.concatenate([low[:24, :256], high[:24, :256]], axis=1),
        jnp.concatenate([low[:24, 256:], high[:24, 256:]], axis=1),
        grad_o,
    )


def solution(mesh):
    torus = Mesh(mesh.devices.reshape(4, 8, 2, 2, 2), AXES)
    return jax.shard_map(
        body,
        mesh=torus,
        in_specs=(P(DP, SEQ, None), P(DP, SEQ, None), P(), P(), P()),
        out_specs=(
            P(DP, SEQ, None),
            P(DP, SEQ, None),
            P(SEQ, None),
            P(SEQ, None),
            P(SEQ, None),
        ),
        check_vma=False,
    )
```
